512 devices in a mesh: sp: 128 (over y, z, core), tp: 4 (over x).
Axes of the slice: x: 4, y: 8, z: 8, core: 2. Of those that a mesh axis runs over, the one named last changes fastest.
Arguments:
- prefilled_block_keys: bfloat16 [8192, 8, 1024], P(('sp', 'tp')), may hold values from -4 to 4
- prefilled_block_values: bfloat16 [8192, 8, 1024], P(('sp', 'tp')), may hold values from -6 to 6
- queries: bfloat16 [4, 4, 8192], P(None, None, 'tp'), may hold values from -128 to 128
- step_token_keys: bfloat16 [4, 4, 1024], P(None, None, 'tp'), may hold values from -32 to 32
- step_token_values: bfloat16 [4, 4, 1024], P(None, None, 'tp'), may hold values from -6 to 6
- lengths: int32 [4], replicated, may hold values from 8185 to 40960, as said below
- block_request: int32 [8192], P(('sp', 'tp')), may hold values from 0 to 3, as said below
- block_number: int32 [8192], P(('sp', 'tp')), may hold values from 0 to 5119
- owner_rank: int32 [8192], P(('sp', 'tp')), may hold values from 0 to 79, as said below
- owner_slot: int32 [8192], P(('sp', 'tp')), may hold values from 0 to 127, as said below
- group_first: int32 [4], replicated, may hold values from 0 to 112, as said below
Outputs:
- attended: float32 [4, 4, 8192], P(None, None, 'tp')
- log_norm: float32 [4, 4, 64], P(None, None, 'tp')
- owner_slot_keys: bfloat16 [16384, 8, 1024], P('sp', None, 'tp')
- owner_slot_values: bfloat16 [16384, 8, 1024], P('sp', None, 'tp')
The draws below stay inside these ranges and needn't reach their ends.
Inputs may be any that keep to these rules, and one draw needn't show every extreme that they name: `lengths`: each request's length lies in its last block: with n blocks, 8 * (n - 1) < length <= 8 * n. `block_request`: every request has blocks, and its blocks carry the numbers 0 to n - 1 once each. The owner group_first + owner_rank lies in the request's group. `owner_slot`: no two blocks share an owner and a slot; the 64 blocks of one index of sp in the prefill layout reach one owner at most 1 times, and this is reached. `group_first`: the groups are runs of indices of sp, one for each request in some order, that do not meet and cover the whole axis.
All inputs are finite; a program needn't handle non-finite values.
Results may differ from the reference program's by a relative error of at most 0.0004.
Values may be sent and summed in bfloat16 or wider, within the bound.
A program may use at most 64 MiB of HBM per device.

```python
import math
import jax
import jax.numpy as jnp
from jax import lax

QUERY_HEADS = 64
KEY_VALUE_HEADS = 8
HEAD_SIZE = 128
DECODE_REQUESTS = 4
DECODE_STEPS = 4
BLOCK_TOKENS = 8
BPD = 16
BLOCK_COUNT = 8192
OWNER_SLOTS = 128
N_SP = 128
N_TP = 4


def block_layout(key):
    key = jax.random.fold_in(key, 101)
    first_key, second_key, third_key, fourth_key, fifth_key, sixth_key, seventh_key = jax.random.split(key, 7)
    row_blocks = BPD * N_TP
    pair_count = N_SP // 2
    spread = jax.random.randint(first_key, (pair_count,), 0, row_blocks)
    forced = jax.random.randint(second_key, (), 0, pair_count)
    spread = jnp.where(jnp.arange(pair_count) == forced, row_blocks, spread)
    flip_bits = jax.random.randint(third_key, (pair_count,), 0, 2)
    signed = spread * (1 - 2 * flip_bits)
    block_loads = jnp.stack([row_blocks + signed, row_blocks - signed], axis=1).reshape(N_SP).astype(jnp.int32)
    run_ends = jnp.cumsum(block_loads)
    run_starts = run_ends - block_loads
    base_pairs = max(1, pair_count // (2 * DECODE_REQUESTS))
    extra_pairs = pair_count - DECODE_REQUESTS * base_pairs
    biggest_place = jax.random.randint(fourth_key, (), 0, DECODE_REQUESTS - 1)
    place_sizes = (2 * (base_pairs + jnp.where(jnp.arange(DECODE_REQUESTS) == biggest_place, extra_pairs, 0))).astype(jnp.int32)
    place_first = (jnp.cumsum(place_sizes) - place_sizes).astype(jnp.int32)
    request_at_place = jax.random.permutation(sixth_key, DECODE_REQUESTS).astype(jnp.int32)
    group_first = jnp.zeros((DECODE_REQUESTS,), jnp.int32).at[request_at_place].set(place_first)
    is_big = jnp.arange(DECODE_REQUESTS) == request_at_place[biggest_place]
    is_shortest = jnp.arange(DECODE_REQUESTS) == request_at_place[(biggest_place + 1) % DECODE_REQUESTS]
    total_blocks = BPD * N_SP * N_TP
    deal_order = jnp.arange(total_blocks, dtype=jnp.int32)
    owner_of_deal = jnp.sum(deal_order[:, None] >= run_ends[None, :], axis=1).astype(jnp.int32)
    slot_of_deal = deal_order - run_starts[owner_of_deal]
    place_of_owner = jnp.sum(jnp.arange(N_SP)[:, None] >= place_first[None, 1:], axis=1).astype(jnp.int32)
    request_of_owner = request_at_place[place_of_owner]
    request_of_deal = request_of_owner[owner_of_deal]
    request_begin = run_starts[group_first]
    number_of_deal = deal_order - request_begin[request_of_deal]
    rank_of_deal = owner_of_deal - group_first[request_of_deal]
    blocks = jnp.arange(total_blocks, dtype=jnp.int32)
    row_keys = jax.random.split(seventh_key, N_SP)
    within_row = jax.vmap(lambda k: jax.random.permutation(k, row_blocks))(row_keys).astype(jnp.int32)
    block_row = blocks // row_blocks
    deal_of_block = within_row[block_row, blocks % row_blocks] * N_SP + block_row
    counts = jnp.sum(jnp.where(request_of_owner[None, :] == jnp.arange(DECODE_REQUESTS)[:, None], block_loads[None, :], 0), axis=1)
    last_fill = jnp.where(is_big, BLOCK_TOKENS, jnp.where(is_shortest, 1, jax.random.randint(fifth_key, (DECODE_REQUESTS,), 1, BLOCK_TOKENS + 1)))
    lengths = BLOCK_TOKENS * (counts - 1) + last_fill
    return (lengths.astype(jnp.int32), request_of_deal[deal_of_block], number_of_deal[deal_of_block], rank_of_deal[deal_of_block], slot_of_deal[deal_of_block], group_first)


def query_draw(key):
    return jax.random.normal(jax.random.fold_in(key, 303), (DECODE_STEPS, DECODE_REQUESTS, QUERY_HEADS * HEAD_SIZE), jnp.float32)


def key_field(key, plant):
    layout = block_layout(key)
    field_key = jax.random.fold_in(key, 202)
    root_random_key = jax.random.fold_in(field_key, 0)
    total_blocks = BPD * N_SP * N_TP
    value_entries = jnp.clip(jax.random.normal(root_random_key, (total_blocks, BLOCK_TOKENS, KEY_VALUE_HEADS * HEAD_SIZE), jnp.float32), -4.0, 4.0)
    positions = layout[2][:, None] * BLOCK_TOKENS + jnp.arange(BLOCK_TOKENS, dtype=jnp.int32)[None, :]
    beyond = positions >= layout[0][layout[1]][:, None]
    lead_heads = query_draw(key).reshape(DECODE_STEPS, DECODE_REQUESTS, KEY_VALUE_HEADS, QUERY_HEADS // KEY_VALUE_HEADS, HEAD_SIZE)[:, :, :, 0, :]
    lead_heads = lead_heads.reshape(DECODE_STEPS, DECODE_REQUESTS, KEY_VALUE_HEADS * HEAD_SIZE)
    step_pick = (jnp.arange(BLOCK_TOKENS, dtype=jnp.int32) % DECODE_STEPS)[None, :]
    tail_rows = jnp.clip(3.0 * lead_heads[step_pick, layout[1][:, None]], -4.0, 4.0)
    value_entries = jnp.where(beyond[..., None], tail_rows, value_entries)
    firsts_hit = (layout[1][None, :] == jnp.arange(DECODE_REQUESTS)[:, None]) & (layout[2][None, :] == 0)
    firsts = jnp.sum(jnp.where(firsts_hit, jnp.arange(total_blocks)[None, :], 0), axis=1)
    request_index = jnp.arange(DECODE_REQUESTS) % 4
    stretch = 1.0 + plant * jnp.array([0.0, 1.5, 0.75, 0.0], jnp.float32)[request_index]
    leading_part = value_entries[firsts, 0]
    planted = jnp.clip(leading_part * stretch[:, None], -4.0, 4.0)
    second = value_entries[firsts, 1]
    blended = jnp.clip(second, -4.0, 4.0)
    value_entries = value_entries.at[firsts, 0].set(planted)
    value_entries = value_entries.at[firsts, 1].set(blended)
    return value_entries


def draw_prefilled_block_keys(key, part):
    plant = 0.0
    value_entries = key_field(key, plant)
    return value_entries.astype(jnp.bfloat16)


def draw_queries(key, part):
    query_matrix = query_draw(key)
    return query_matrix.astype(jnp.bfloat16)


def draw_step_token_keys(key, part):
    query_matrix = query_draw(key)
    key = jax.random.fold_in(key, 9)
    head_grouped = jnp.mean(query_matrix.reshape(DECODE_STEPS, DECODE_REQUESTS, KEY_VALUE_HEADS, QUERY_HEADS // KEY_VALUE_HEADS, HEAD_SIZE), axis=3)
    noise_amplitude = 9.0 * (QUERY_HEADS // KEY_VALUE_HEADS) / math.sqrt(HEAD_SIZE)
    random_rows = 0.5 * jax.random.normal(key, head_grouped.shape, jnp.float32)
    return jnp.clip(head_grouped * noise_amplitude + random_rows, -32.0, 32.0).reshape(DECODE_STEPS, DECODE_REQUESTS, KEY_VALUE_HEADS * HEAD_SIZE).astype(jnp.bfloat16)


def draw_lengths(key, part):
    return block_layout(key)[0]


def draw_block_request(key, part):
    return block_layout(key)[1]


def draw_block_number(key, part):
    return block_layout(key)[2]


def draw_owner_rank(key, part):
    return block_layout(key)[3]


def draw_owner_slot(key, part):
    return block_layout(key)[4]


def draw_group_first(key, part):
    return block_layout(key)[5]


def shard_levels(key, extent, pieces, least, top_value):
    def one(dim, parts):
        heights = jax.random.uniform(jax.random.fold_in(jax.random.fold_in(key, 6), dim), (parts,), jnp.float32, least / len(pieces), top_value / len(pieces))
        return jnp.repeat(jnp.exp(heights), extent[dim] // parts).reshape((-1,) + (1,) * (len(extent) - dim - 1))

    factor_of = one(*pieces[0])
    for cut in pieces[1:]:
        factor_of = factor_of * one(*cut)
    return factor_of


def scatter_about(rng, shape, deviation, limit, cuts=(), kind=jnp.bfloat16):
    values = jax.random.normal(rng, shape, jnp.float32) * deviation
    if len(cuts) > 0:
        values = shard_levels(rng, shape, cuts, -0.22, 0.18) * values
    return jnp.clip(values, min=-limit, max=limit).astype(kind)


def setup_inputs(seed: int = 0) -> dict:
    streams_of = jax.random.split(jax.random.key(seed), 12)
    return {
        "prefilled_block_keys": draw_prefilled_block_keys(jax.random.fold_in(streams_of[11], 71), 0),
        "prefilled_block_values": scatter_about(streams_of[1], (BLOCK_COUNT, BLOCK_TOKENS, KEY_VALUE_HEADS * HEAD_SIZE), 1.0, 6.0, ((0, 512),)),
        "queries": draw_queries(jax.random.fold_in(streams_of[11], 71), 0),
        "step_token_keys": draw_step_token_keys(jax.random.fold_in(streams_of[11], 71), 0),
        "step_token_values": scatter_about(streams_of[4], (DECODE_STEPS, DECODE_REQUESTS, KEY_VALUE_HEADS * HEAD_SIZE), 1.0, 6.0, ((2, 4),)),
        "lengths": draw_lengths(jax.random.fold_in(streams_of[11], 71), 0),
        "block_request": draw_block_request(jax.random.fold_in(streams_of[11], 71), 0),
        "block_number": draw_block_number(jax.random.fold_in(streams_of[11], 71), 0),
        "owner_rank": draw_owner_rank(jax.random.fold_in(streams_of[11], 71), 0),
        "owner_slot": draw_owner_slot(jax.random.fold_in(streams_of[11], 71), 0),
        "group_first": draw_group_first(jax.random.fold_in(streams_of[11], 71), 0),
    }


NEGATIVE = -1e+30

def reference(prefilled_block_keys, prefilled_block_values, queries, step_token_keys, step_token_values, lengths, block_request, block_number, owner_rank, owner_slot, group_first):
    owners = group_first[block_request] + owner_rank
    expected_output = owners * OWNER_SLOTS + owner_slot
    owner_slot_keys = jnp.zeros((N_SP * OWNER_SLOTS, BLOCK_TOKENS, KEY_VALUE_HEADS * HEAD_SIZE), jnp.bfloat16).at[expected_output].add(prefilled_block_keys)
    owner_slot_values = jnp.zeros((N_SP * OWNER_SLOTS, BLOCK_TOKENS, KEY_VALUE_HEADS * HEAD_SIZE), jnp.bfloat16).at[expected_output].add(prefilled_block_values)
    queries_per_group = QUERY_HEADS // KEY_VALUE_HEADS
    score_scale = 1.0 / math.sqrt(HEAD_SIZE)
    token_request = jnp.repeat(block_request, BLOCK_TOKENS)
    token_position = (block_number[:, None] * BLOCK_TOKENS + jnp.arange(BLOCK_TOKENS, dtype=jnp.int32)[None, :]).reshape(-1)
    within_length = token_position < lengths[token_request]
    member = token_request[None, :] == jnp.arange(DECODE_REQUESTS, dtype=jnp.int32)[:, None]
    allowed_mask = member & within_length[None, :]
    key_matrix = prefilled_block_keys.reshape(-1, KEY_VALUE_HEADS, HEAD_SIZE)
    value_matrix = prefilled_block_values.reshape(-1, KEY_VALUE_HEADS, HEAD_SIZE)
    query_matrix = queries.reshape(DECODE_STEPS, DECODE_REQUESTS, KEY_VALUE_HEADS, queries_per_group, HEAD_SIZE)
    current_keys = step_token_keys.reshape(DECODE_STEPS, DECODE_REQUESTS, KEY_VALUE_HEADS, HEAD_SIZE)
    current_values = step_token_values.reshape(DECODE_STEPS, DECODE_REQUESTS, KEY_VALUE_HEADS, HEAD_SIZE)
    causal = jnp.arange(DECODE_STEPS)[None, :] <= jnp.arange(DECODE_STEPS)[:, None]

    def single_head(head_index):
        query_head = lax.dynamic_index_in_dim(query_matrix, head_index, 2, keepdims=False).astype(jnp.float32)
        key_head = lax.dynamic_index_in_dim(key_matrix, head_index, 1, keepdims=False).astype(jnp.float32)
        value_head = lax.dynamic_index_in_dim(value_matrix, head_index, 1, keepdims=False).astype(jnp.float32)
        fresh_key_head = lax.dynamic_index_in_dim(current_keys, head_index, 2, keepdims=False).astype(jnp.float32)
        fresh_value_head = lax.dynamic_index_in_dim(current_values, head_index, 2, keepdims=False).astype(jnp.float32)
        scores = jnp.einsum('srgd,td->srgt', query_head, key_head, precision=lax.Precision.HIGHEST) * score_scale
        fresh_scores = jnp.einsum('srgd,jrd->srgj', query_head, fresh_key_head, precision=lax.Precision.HIGHEST) * score_scale
        cache_allowed = allowed_mask[None, :, None, :]
        fresh_allowed = causal[:, None, None, :]
        row_top = jnp.maximum(lax.optimization_barrier(jnp.max(jnp.where(cache_allowed, scores, NEGATIVE), axis=-1)), lax.optimization_barrier(jnp.max(jnp.where(fresh_allowed, fresh_scores, NEGATIVE), axis=-1)))
        weights = jnp.where(cache_allowed, jnp.exp(scores - row_top[..., None]), 0.0)
        fresh_weights = jnp.where(fresh_allowed, jnp.exp(fresh_scores - row_top[..., None]), 0.0)
        weight_sum = lax.optimization_barrier(jnp.sum(weights, axis=-1)) + lax.optimization_barrier(jnp.sum(fresh_weights, axis=-1))
        rounded = lax.optimization_barrier(weights.astype(jnp.bfloat16)).astype(jnp.float32)
        fresh_rounded = lax.optimization_barrier(fresh_weights.astype(jnp.bfloat16)).astype(jnp.float32)
        numerator = jnp.einsum('srgt,td->srgd', rounded, value_head, precision=lax.Precision.HIGHEST)
        numerator = numerator + jnp.einsum('srgj,jrd->srgd', fresh_rounded, fresh_value_head, precision=lax.Precision.HIGHEST)
        return (numerator / weight_sum[..., None], row_top + jnp.log(weight_sum))
    output_rows, norm_logarithms = lax.map(single_head, jnp.arange(KEY_VALUE_HEADS, dtype=jnp.int32))
    attended = output_rows.transpose(1, 2, 0, 3, 4).reshape(DECODE_STEPS, DECODE_REQUESTS, QUERY_HEADS * HEAD_SIZE)
    log_norm = norm_logarithms.transpose(1, 2, 0, 3).reshape(DECODE_STEPS, DECODE_REQUESTS, QUERY_HEADS)
    return (attended, log_norm, owner_slot_keys, owner_slot_values)
```

```python
import functools
import math

import jax
import jax.numpy as jnp
from jax import lax
from jax.experimental import pallas as pl
from jax.experimental.pallas import tpu as pltpu
from jax.sharding import PartitionSpec as P

D = 128
TOK = 8
STEPS = 4
REQUESTS = 4
SR = STEPS * REQUESTS
GROUP = 8
ROWS = GROUP * SR
LOCAL_HEADS = 2
PIECE = LOCAL_HEADS * D
NEGATIVE = -1e30
SCALE = 1.0 / math.sqrt(D)
MESH = pl.DeviceIdType.MESH
F32 = jnp.float32
BF16 = jnp.bfloat16
NT = (((1,), (1,)), ((), ()))
TN = (((0,), (0,)), ((), ()))


def exchange_kernel(
    n_y,
    n_zc,
    n_tp,
    own_blocks,
    request_ref,
    number_ref,
    rank_ref,
    slot_ref,
    lengths_ref,
    first_ref,
    q_ref,
    fresh_k_ref,
    fresh_v_ref,
    keys_ref,
    values_ref,
    attended_ref,
    norm_ref,
    arrival_ref,
    kc,
    vc,
    meta,
    kp,
    vp,
    k32,
    v32,
    src_v,
    src_s,
    scores,
    ka,
    kb,
    va,
    vb,
    mx,
    my_msg,
    my_buf,
    fresh_num,
    rs_src,
    rs_buf,
    yy_buf,
    ag_buf,
    local_sem,
    meta_send,
    meta_recv,
    kp_send,
    kp_recv,
    vp_send,
    vp_recv,
    mx_send,
    mx_recv,
    my_send,
    my_recv,
    k1_send,
    k1_recv,
    k2_send,
    k2_recv,
    v1_send,
    v1_recv,
    v2_send,
    v2_recv,
    rs_send,
    rs_recv,
    yy_send,
    yy_recv,
    ag_send,
    ag_recv,
):
    me = lax.axis_index("sp")
    tp = lax.axis_index("tp")
    my = me // n_zc
    mzc = lax.rem(me, n_zc)
    tokens = own_blocks * TOK

    def zc_at(k):
        return lax.rem(mzc + k, n_zc)

    def y_at(j):
        return lax.rem(my + j, n_y)

    def tp_at(k):
        return lax.rem(tp + k, n_tp)

    def zc_dev(k):
        return (my * n_zc + zc_at(k), tp)

    def y_dev(j):
        return (y_at(j) * n_zc + mzc, tp)

    def tp_dev(k):
        return (me, tp_at(k))

    def remote(src, dst, send, recv, dev):
        copy = pltpu.make_async_remote_copy(
            src_ref=src, dst_ref=dst, send_sem=send, recv_sem=recv, device_id=dev, device_id_type=MESH
        )
        copy.start()
        return copy

    barrier = pltpu.get_barrier_semaphore()
    for k in range(1, n_tp):
        pl.semaphore_signal(barrier, inc=1, device_id=tp_dev(k), device_id_type=MESH)
    for k in range(1, n_zc):
        pl.semaphore_signal(barrier, inc=1, device_id=zc_dev(k), device_id_type=MESH)
    for j in range(1, n_y):
        pl.semaphore_signal(barrier, inc=1, device_id=y_dev(j), device_id_type=MESH)

    def columns(t):
        return pl.ds(pl.multiple_of(t * PIECE, PIECE), PIECE)

    own_k = pltpu.make_async_copy(keys_ref.at[:, columns(tp)], kp.at[tp], local_sem.at[0])
    own_v = pltpu.make_async_copy(values_ref.at[:, columns(tp)], vp.at[tp], local_sem.at[1])
    own_k.start()
    own_v.start()

    lane = lax.broadcasted_iota(jnp.int32, (1, D), 1)
    codes = jnp.full((1, D), REQUESTS, jnp.int32)
    sources = jnp.zeros((1, D), jnp.int32)
    slots = jnp.zeros((1, D), jnp.int32)
    for b in range(own_blocks):
        request = request_ref[b]
        owner = first_ref[request] + rank_ref[b]
        place = number_ref[b] * TOK + (lane - b * TOK)
        mine = (lane >= b * TOK) & (lane < (b + 1) * TOK) & (place < lengths_ref[request])
        codes = jnp.where(mine, request, codes)
        hit = lane == owner
        sources = jnp.where(hit, tp * own_blocks + b + 1, sources)
        slots = jnp.where(hit, slot_ref[b] + 1, slots)
    own_meta = jnp.concatenate(
        [codes, sources, slots, jnp.zeros((5, D), jnp.int32)], axis=0
    )
    meta[tp] = own_meta

    row_lane = lax.broadcasted_iota(jnp.int32, (1, ROWS), 1)
    row_request = lax.rem(row_lane, REQUESTS)
    row_step = lax.rem(row_lane, SR) // REQUESTS
    row_code = row_request.astype(F32)

    def q_head(h):
        return jnp.concatenate(
            [q_ref[:, pl.ds((h * GROUP + g) * D, D)] for g in range(GROUP)], axis=0
        )

    fresh_row = lax.broadcasted_iota(jnp.int32, (SR, ROWS), 0)
    fresh_ok = (lax.rem(fresh_row, REQUESTS) == row_request) & (fresh_row // REQUESTS <= row_step)
    fresh_scores = []
    for h in range(LOCAL_HEADS):
        dots = lax.dot_general(
            fresh_k_ref[:, pl.ds(h * D, D)], q_head(h), NT, preferred_element_type=F32
        )
        fresh_scores.append(jnp.where(fresh_ok, dots * SCALE, NEGATIVE))

    k32[0] = jnp.zeros((TOK, PIECE), F32)
    v32[0] = jnp.zeros((TOK, PIECE), F32)

    pl.semaphore_wait(barrier, n_tp - 1 + n_zc - 1 + n_y - 1)

    meta_copies, k_copies, v_copies = [], [], []
    for k in range(1, n_tp):
        meta_copies.append(
            remote(meta.at[tp], meta.at[tp], meta_send.at[k], meta_recv.at[k], tp_dev(k))
        )
    for k in range(1, n_tp):
        k_copies.append(
            remote(keys_ref.at[:, columns(tp_at(k))], kp.at[tp], kp_send.at[k], kp_recv.at[k], tp_dev(k))
        )
    for k in range(1, n_tp):
        v_copies.append(
            remote(
                values_ref.at[:, columns(tp_at(k))], vp.at[tp], vp_send.at[k], vp_recv.at[k], tp_dev(k)
            )
        )

    for copy in meta_copies:
        copy.wait_recv()
    row_meta = meta[0]
    for t in range(1, n_tp):
        row_meta = jnp.maximum(row_meta, meta[t])
    src_v[...] = row_meta
    to_scalar = pltpu.make_async_copy(src_v, src_s, local_sem.at[2])
    to_scalar.start()
    code_columns = [
        jnp.transpose(jnp.broadcast_to(meta[t][0:1, :].astype(F32), (D, D)))[:tokens, :] for t in range(n_tp)
    ]

    own_k.wait()
    for copy in k_copies:
        copy.wait_recv()
    tops = []
    for h in range(LOCAL_HEADS):
        q_rows = q_head(h)
        top = jnp.full((1, ROWS), NEGATIVE, F32)
        for t in range(n_tp):
            dots = lax.dot_general(
                kp[t, :, pl.ds(h * D, D)], q_rows, NT, preferred_element_type=F32
            )
            masked = jnp.where(code_columns[t] == row_code, dots * SCALE, NEGATIVE)
            scores[h, pl.ds(t * tokens, tokens), :] = masked
            top = jnp.maximum(top, jnp.max(masked, axis=0, keepdims=True))
        tops.append(top)
    mx[0] = jnp.concatenate(tops + [row_meta[2:3, :].astype(F32), jnp.zeros((5, D), F32)], axis=0)
    mx_copies = [
        remote(mx.at[0], mx.at[k], mx_send.at[k], mx_recv.at[k], zc_dev(k)) for k in range(1, n_zc)
    ]

    def block_tile(ref, index):
        block = ref[index]
        return jnp.concatenate([block[:, :D], block[:, D:]], axis=0).astype(BF16)

    def source_of(k, j):
        return src_s[1, y_at(j) * n_zc + zc_at(k)]

    for t in range(n_tp):
        k32[pl.ds(1 + t * own_blocks, own_blocks)] = kp[t].astype(F32).reshape(own_blocks, TOK, PIECE)
    to_scalar.wait()

    k1_copies = []
    for k in list(range(1, n_zc)) + [0]:
        for j in range(n_y):
            tile = block_tile(k32, source_of(k, j))
            if k == 0:
                kb[0, j] = tile
            else:
                ka[k, j] = tile
        if k > 0:
            k1_copies.append(remote(ka.at[k], kb.at[k], k1_send.at[k], k1_recv.at[k], zc_dev(k)))

    own_v.wait()
    for copy in v_copies:
        copy.wait_recv()
    for t in range(n_tp):
        v32[pl.ds(1 + t * own_blocks, own_blocks)] = vp[t].astype(F32).reshape(own_blocks, TOK, PIECE)
    v1_copies = []
    for j in list(range(1, n_y)) + [0]:
        for k in range(n_zc):
            tile = block_tile(v32, source_of(k, j))
            if j == 0:
                vb[0, k] = tile
            else:
                va[j, k] = tile
        if j > 0:
            v1_copies.append(remote(va.at[j], vb.at[j], v1_send.at[j], v1_recv.at[j], y_dev(j)))

    for copy in mx_copies:
        copy.wait_recv()
    tile_max = mx[0]
    for k in range(1, n_zc):
        tile_max = jnp.maximum(tile_max, mx[k])
    for k in range(n_zc):
        my_buf[0, pl.ds(k, 1), :] = mx[k, pl.ds(2, 1), :]
    my_buf[0, pl.ds(n_zc, 8), :] = tile_max
    my_copies = [
        remote(my_buf.at[0], my_buf.at[j], my_send.at[j], my_recv.at[j], y_dev(j))
        for j in range(1, n_y)
    ]
    for copy in my_copies:
        copy.wait_recv()
    all_max = my_buf[0, pl.ds(n_zc, 8), :]
    for j in range(1, n_y):
        all_max = jnp.maximum(all_max, my_buf[j, pl.ds(n_zc, 8), :])

    chunk = D // n_zc
    row_tops = []
    for h in range(LOCAL_HEADS):
        row_top = jnp.maximum(
            all_max[h : h + 1, :], jnp.max(fresh_scores[h], axis=0, keepdims=True)
        )
        row_tops.append(row_top)
        total = jnp.zeros((1, ROWS), F32)
        number = jnp.zeros((D, ROWS), F32)
        for t in range(n_tp):
            weights = jnp.exp(scores[h, pl.ds(t * tokens, tokens), :] - row_top)
            total = total + jnp.sum(weights, axis=0, keepdims=True)
            number = number + lax.dot_general(
                vp[t, :, pl.ds(h * D, D)], weights.astype(BF16), TN, preferred_element_type=F32
            )
        for p in range(n_zc):
            rs_src[p, pl.ds(h * chunk, chunk), :] = number[p * chunk : (p + 1) * chunk, :]
            rs_src[p, pl.ds(LOCAL_HEADS * chunk + h, 1), :] = total
    rs_copies = []
    for k in range(1, n_zc):
        rs_copies.append(
            remote(rs_src.at[zc_at(k)], rs_buf.at[mzc], rs_send.at[k], rs_recv.at[k], zc_dev(k))
        )
    rs_buf[mzc] = rs_src[mzc]

    fresh_totals = []
    for h in range(LOCAL_HEADS):
        weights = jnp.exp(fresh_scores[h] - row_tops[h])
        fresh_totals.append(jnp.sum(weights, axis=0, keepdims=True))
        number = lax.dot_general(
            fresh_v_ref[:, pl.ds(h * D, D)], weights.astype(BF16), TN, preferred_element_type=F32
        )
        for p in range(n_zc):
            fresh_num[p, pl.ds(h * chunk, chunk), :] = number[p * chunk : (p + 1) * chunk, :]

    column = []
    for j in range(n_y):
        lists = my_buf[j, pl.ds(0, n_zc), :]
        wide = lax.broadcasted_iota(jnp.int32, (n_zc, D), 1)
        picked = jnp.sum(jnp.where(wide == me, lists, 0.0), axis=1, keepdims=True)
        index = lax.broadcasted_iota(jnp.int32, (n_zc, D), 0) + (j * n_zc + 1)
        found = jnp.where(picked == (wide + 1).astype(F32), index, 0)
        column.append(jnp.sum(found, axis=0, keepdims=True))
    arrival = column[0]
    for j in range(1, n_y):
        arrival = arrival + column[j]
    arrival_ref[...] = jnp.broadcast_to(arrival, (8, D))

    k2_copies = []
    for copy in k1_copies:
        copy.wait_recv()
    for j in range(1, n_y):
        k2_copies.append(remote(kb.at[:, j], kc.at[j], k2_send.at[j], k2_recv.at[j], y_dev(j)))
    own_k2 = pltpu.make_async_copy(kb.at[:, 0], kc.at[0], local_sem.at[3])
    own_k2.start()

    for copy in rs_copies:
        copy.wait_recv()
    part = rs_buf[0]
    for p in range(1, n_zc):
        part = part + rs_buf[p]
    yy_buf[my] = part
    yy_copies = [
        remote(yy_buf.at[my], yy_buf.at[my], yy_send.at[j], yy_recv.at[j], y_dev(j))
        for j in range(1, n_y)
    ]

    v2_copies = []
    for copy in v1_copies:
        copy.wait_recv()
    for k in range(1, n_zc):
        v2_copies.append(remote(vb.at[:, k], vc.at[:, k], v2_send.at[k], v2_recv.at[k], zc_dev(k)))
    own_v2 = pltpu.make_async_copy(vb.at[:, 0], vc.at[:, 0], local_sem.at[4])
    own_v2.start()

    for copy in yy_copies:
        copy.wait_recv()
    whole = yy_buf[0]
    for j in range(1, n_y):
        whole = whole + yy_buf[j]
    norms = []
    for h in range(LOCAL_HEADS):
        total = whole[LOCAL_HEADS * chunk + h : LOCAL_HEADS * chunk + h + 1, :] + fresh_totals[h]
        number = whole[h * chunk : (h + 1) * chunk, :] + fresh_num[mzc, pl.ds(h * chunk, chunk), :]
        ag_buf[mzc, pl.ds(h * chunk, chunk), :] = number / total
        norms.append(row_tops[h] + jnp.log(total))
    norm_ref[...] = jnp.concatenate(norms + [jnp.zeros((6, ROWS), F32)], axis=0)
    ag_copies = [
        remote(ag_buf.at[mzc], ag_buf.at[mzc], ag_send.at[k], ag_recv.at[k], zc_dev(k))
        for k in range(1, n_zc)
    ]
    for copy in ag_copies:
        copy.wait_recv()
    for h in range(LOCAL_HEADS):
        by_entry = jnp.concatenate(
            [ag_buf[p, pl.ds(h * chunk, chunk), :] for p in range(n_zc)], axis=0
        )
        by_row = jnp.transpose(by_entry)
        for g in range(GROUP):
            attended_ref[:, pl.ds((h * GROUP + g) * D, D)] = by_row[g * SR : (g + 1) * SR, :]

    for copy in k2_copies + v2_copies:
        copy.wait_recv()
    own_k2.wait()
    own_v2.wait()
    for copy in (
        meta_copies
        + k_copies
        + v_copies
        + mx_copies
        + my_copies
        + k1_copies
        + v1_copies
        + k2_copies
        + v2_copies
        + rs_copies
        + yy_copies
        + ag_copies
    ):
        copy.wait_send()


def place_kernel(slot_count, arrival_ref, k_ref, v_ref, out_k_ref, out_v_ref):
    def place(s, carry):
        index = arrival_ref[s]
        at = jnp.maximum(index - 1, 0)
        there = index > 0
        for ref, out in ((k_ref, out_k_ref), (v_ref, out_v_ref)):
            tile = ref[at].astype(F32)
            wide = jnp.concatenate([tile[:TOK, :], tile[TOK:, :]], axis=1)
            out[s] = jnp.where(there, wide, 0.0).astype(BF16)
        return carry

    lax.fori_loop(0, slot_count, place, 0, unroll=4)


def on_device(
    n_y,
    n_zc,
    prefilled_block_keys,
    prefilled_block_values,
    queries,
    step_token_keys,
    step_token_values,
    lengths,
    block_request,
    block_number,
    owner_rank,
    owner_slot,
    group_first,
):
    n_tp = lax.axis_size("tp")
    own_blocks, _, full_width = prefilled_block_keys.shape
    row_blocks = own_blocks * n_tp
    tokens = own_blocks * TOK
    slot_count = 2 * row_blocks
    n_sp = n_y * n_zc
    chunk = D // n_zc
    rs_rows = LOCAL_HEADS * chunk + 8
    smem = pl.BlockSpec(memory_space=pltpu.SMEM)
    vmem = pl.BlockSpec(memory_space=pltpu.VMEM)
    hbm = pl.BlockSpec(memory_space=pl.ANY)
    dma = pltpu.SemaphoreType.DMA
    attended, norms, arrival, kc, vc = pl.pallas_call(
        functools.partial(exchange_kernel, n_y, n_zc, n_tp, own_blocks),
        out_shape=(
            jax.ShapeDtypeStruct((SR, GROUP * PIECE), F32),
            jax.ShapeDtypeStruct((8, ROWS), F32),
            jax.ShapeDtypeStruct((8, D), jnp.int32),
            jax.ShapeDtypeStruct((n_y, n_zc, 2 * TOK, D), BF16),
            jax.ShapeDtypeStruct((n_y, n_zc, 2 * TOK, D), BF16),
        ),
        in_specs=[smem] * 6 + [vmem] * 3 + [hbm] * 2,
        out_specs=(vmem,) * 5,
        scratch_shapes=[
            pltpu.VMEM((n_tp, 8, D), jnp.int32),
            pltpu.VMEM((n_tp, tokens, PIECE), BF16),
            pltpu.VMEM((n_tp, tokens, PIECE), BF16),
            pltpu.VMEM((row_blocks + 1, TOK, PIECE), F32),
            pltpu.VMEM((row_blocks + 1, TOK, PIECE), F32),
            pltpu.VMEM((8, D), jnp.int32),
            pltpu.SMEM((8, D), jnp.int32),
            pltpu.VMEM((LOCAL_HEADS, n_tp * tokens, ROWS), F32),
            pltpu.VMEM((n_zc, n_y, 2 * TOK, D), BF16),
            pltpu.VMEM((n_zc, n_y, 2 * TOK, D), BF16),
            pltpu.VMEM((n_y, n_zc, 2 * TOK, D), BF16),
            pltpu.VMEM((n_y, n_zc, 2 * TOK, D), BF16),
            pltpu.VMEM((n_zc, 8, D), F32),
            pltpu.VMEM((8, D), F32),
            pltpu.VMEM((n_y, n_zc + 8, D), F32),
            pltpu.VMEM((n_zc, LOCAL_HEADS * chunk, ROWS), F32),
            pltpu.VMEM((n_zc, rs_rows, ROWS), F32),
            pltpu.VMEM((n_zc, rs_rows, ROWS), F32),
            pltpu.VMEM((n_y, rs_rows, ROWS), F32),
            pltpu.VMEM((n_zc, LOCAL_HEADS * chunk, ROWS), F32),
            dma((5,)),
        ]
        + [dma((n_tp,))] * 6
        + [dma((n_zc,))] * 2
        + [dma((n_y,))] * 2
        + [dma((n_zc,))] * 2
        + [dma((n_y,))] * 2
        + [dma((n_y,))] * 2
        + [dma((n_zc,))] * 2
        + [dma((n_zc,))] * 2
        + [dma((n_y,))] * 2
        + [dma((n_zc,))] * 2,
        compiler_params=pltpu.CompilerParams(
            collective_id=0, has_side_effects=True, vmem_limit_bytes=40 * 2**20
        ),
        name="exchange",
    )(
        block_request,
        block_number,
        owner_rank,
        owner_slot,
        lengths,
        group_first,
        queries.reshape(SR, GROUP * PIECE),
        step_token_keys.reshape(SR, PIECE),
        step_token_values.reshape(SR, PIECE),
        prefilled_block_keys.reshape(tokens, full_width),
        prefilled_block_values.reshape(tokens, full_width),
    )
    slot_shape = jax.ShapeDtypeStruct((slot_count, TOK, PIECE), BF16)
    owner_slot_keys, owner_slot_values = pl.pallas_call(
        functools.partial(place_kernel, slot_count),
        out_shape=(slot_shape, slot_shape),
        in_specs=[smem, vmem, vmem],
        out_specs=(vmem, vmem),
        compiler_params=pltpu.CompilerParams(vmem_limit_bytes=16 * 2**20),
        name="place",
    )(
        arrival[0],
        kc.reshape(n_sp, 2 * TOK, D),
        vc.reshape(n_sp, 2 * TOK, D),
    )
    log_norm = (
        norms[:LOCAL_HEADS]
        .reshape(LOCAL_HEADS, GROUP, STEPS, REQUESTS)
        .transpose(2, 3, 0, 1)
        .reshape(STEPS, REQUESTS, LOCAL_HEADS * GROUP)
    )
    return (
        attended.reshape(STEPS, REQUESTS, GROUP * PIECE),
        log_norm,
        owner_slot_keys,
        owner_slot_values,
    )


def solution(mesh):
    sp = mesh.shape["sp"]
    n_y = max(2, sp // 16)
    return jax.shard_map(
        functools.partial(on_device, n_y, sp // n_y),
        mesh=mesh,
        in_specs=(
            P(("sp", "tp"), None, None),
            P(("sp", "tp"), None, None),
            P(None, None, "tp"),
            P(None, None, "tp"),
            P(None, None, "tp"),
            P(),
            P(("sp", "tp")),
            P(("sp", "tp")),
            P(("sp", "tp")),
            P(("sp", "tp")),
            P(),
        ),
        out_specs=(
            P(None, None, "tp"),
            P(None, None, "tp"),
            P("sp", None, "tp"),
            P("sp", None, "tp"),
        ),
        check_vma=False,
    )
```

```python
import functools
import math

import jax
import jax.numpy as jnp
from jax import lax
from jax.experimental import pallas as pl
from jax.experimental.pallas import tpu as pltpu
from jax.sharding import PartitionSpec as P

D = 128
TOK = 8
STEPS = 4
REQUESTS = 4
SR = STEPS * REQUESTS
GROUP = 8
ROWS = GROUP * SR
LOCAL_HEADS = 2
PIECE = LOCAL_HEADS * D
NEGATIVE = -1e30
SCALE = 1.0 / math.sqrt(D)
MESH = pl.DeviceIdType.MESH
F32 = jnp.float32
BF16 = jnp.bfloat16
NT = (((1,), (1,)), ((), ()))
TN = (((0,), (0,)), ((), ()))


def exchange_kernel(
    n_y,
    n_zc,
    n_tp,
    own_blocks,
    request_ref,
    number_ref,
    rank_ref,
    slot_ref,
    lengths_ref,
    first_ref,
    q_ref,
    fresh_k_ref,
    fresh_v_ref,
    keys_ref,
    values_ref,
    attended_ref,
    norm_ref,
    arrival_ref,
    kc,
    vc,
    meta,
    kp,
    vp,
    k32,
    v32,
    src_v,
    src_s,
    scores,
    ka,
    kb,
    va,
    vb,
    qs,
    fresh_ks,
    fresh_vs,
    sl,
    sy,
    su,
    sv,
    mx,
    my_buf,
    fresh_num,
    rs_src,
    rs_buf,
    yy_buf,
    ag_buf,
    local_sem,
    meta_send,
    meta_recv,
    kp_send,
    kp_recv,
    vp_send,
    vp_recv,
    sl_send,
    sl_recv,
    sy_send,
    sy_recv,
    su_send,
    su_recv,
    sv_send,
    sv_recv,
    mx_send,
    mx_recv,
    my_send,
    my_recv,
    z_send,
    z_recv,
    y_send,
    y_recv,
    rs_send,
    rs_recv,
    yy_send,
    yy_recv,
    ag_send,
    ag_recv,
):
    me = lax.axis_index("sp")
    tp = lax.axis_index("tp")
    my = me // n_zc
    mzc = lax.rem(me, n_zc)
    tokens = own_blocks * TOK

    def zc_at(k):
        return lax.rem(mzc + k, n_zc)

    def y_at(j):
        return lax.rem(my + j, n_y)

    def tp_at(k):
        return lax.rem(tp + k, n_tp)

    z_order = sorted(range(1, n_zc), key=lambda k: -min(k, n_zc - k))
    y_order = sorted(range(1, n_y), key=lambda j: -min(j, n_y - j))
    odd_order = [(j - 1) // 2 for j in y_order if j % 2]
    even_order = [j // 2 for j in y_order if j % 2 == 0]

    def zc_dev(k):
        return (my * n_zc + zc_at(k), tp)

    def y_dev(j):
        return (y_at(j) * n_zc + mzc, tp)

    def tp_dev(k):
        return (me, tp_at(k))

    def remote(src, dst, send, recv, dev):
        copy = pltpu.make_async_remote_copy(
            src_ref=src, dst_ref=dst, send_sem=send, recv_sem=recv, device_id=dev, device_id_type=MESH
        )
        copy.start()
        return copy

    barrier = pltpu.get_barrier_semaphore()
    for k in range(1, n_tp):
        pl.semaphore_signal(barrier, inc=1, device_id=tp_dev(k), device_id_type=MESH)
    for k in range(1, n_zc):
        pl.semaphore_signal(barrier, inc=1, device_id=zc_dev(k), device_id_type=MESH)
    for j in range(1, n_y):
        pl.semaphore_signal(barrier, inc=1, device_id=y_dev(j), device_id_type=MESH)

    def columns(t):
        return pl.ds(pl.multiple_of(t * PIECE, PIECE), PIECE)

    def rows_of(t):
        return pl.ds(pl.multiple_of(t * tokens, tokens), tokens)

    own_k = pltpu.make_async_copy(keys_ref.at[:, columns(tp)], kp.at[rows_of(tp)], local_sem.at[0])
    own_v = pltpu.make_async_copy(values_ref.at[:, columns(tp)], vp.at[rows_of(tp)], local_sem.at[1])
    own_k.start()
    own_v.start()

    lane = lax.broadcasted_iota(jnp.int32, (1, D), 1)
    codes = jnp.full((1, D), REQUESTS, jnp.int32)
    sources = jnp.zeros((1, D), jnp.int32)
    slots = jnp.zeros((1, D), jnp.int32)
    for b in range(own_blocks):
        request = request_ref[b]
        owner = first_ref[request] + rank_ref[b]
        place = number_ref[b] * TOK + (lane - b * TOK)
        mine = (lane >= b * TOK) & (lane < (b + 1) * TOK) & (place < lengths_ref[request])
        codes = jnp.where(mine, request, codes)
        hit = lane == owner
        sources = jnp.where(hit, tp * own_blocks + b + 1, sources)
        slots = jnp.where(hit, slot_ref[b] + 1, slots)
    own_meta = jnp.concatenate(
        [codes, sources, slots, jnp.zeros((5, D), jnp.int32)], axis=0
    )
    meta[tp] = own_meta

    row_lane = lax.broadcasted_iota(jnp.int32, (1, ROWS), 1)
    row_request = lax.rem(row_lane, REQUESTS)
    row_step = lax.rem(row_lane, SR) // REQUESTS
    row_code = row_request.astype(F32)

    def stack_steps(ref, out):
        out[...] = jnp.concatenate([ref[s].astype(F32) for s in range(STEPS)], axis=0).astype(BF16)

    stack_steps(q_ref, qs)
    stack_steps(fresh_k_ref, fresh_ks)
    stack_steps(fresh_v_ref, fresh_vs)

    def q_head(h):
        return jnp.concatenate(
            [qs[:, pl.ds((h * GROUP + g) * D, D)] for g in range(GROUP)], axis=0
        )

    fresh_row = lax.broadcasted_iota(jnp.int32, (SR, ROWS), 0)
    fresh_ok = (lax.rem(fresh_row, REQUESTS) == row_request) & (fresh_row // REQUESTS <= row_step)
    fresh_scores = []
    for h in range(LOCAL_HEADS):
        dots = lax.dot_general(
            fresh_ks[:, pl.ds(h * D, D)], q_head(h), NT, preferred_element_type=F32
        )
        fresh_scores.append(jnp.where(fresh_ok, dots * SCALE, NEGATIVE))

    k32[0] = jnp.zeros((TOK, PIECE), F32)
    v32[0] = jnp.zeros((TOK, PIECE), F32)

    pl.semaphore_wait(barrier, n_tp - 1 + n_zc - 1 + n_y - 1)

    meta_copies, k_copies, v_copies = [], [], []
    for k in range(1, n_tp):
        meta_copies.append(
            remote(meta.at[tp], meta.at[tp], meta_send.at[k], meta_recv.at[k], tp_dev(k))
        )
    for k in range(1, n_tp):
        k_copies.append(
            remote(keys_ref.at[:, columns(tp_at(k))], kp.at[rows_of(tp)], kp_send.at[k], kp_recv.at[k], tp_dev(k))
        )
    for k in range(1, n_tp):
        v_copies.append(
            remote(
                values_ref.at[:, columns(tp_at(k))], vp.at[rows_of(tp)], vp_send.at[k], vp_recv.at[k], tp_dev(k)
            )
        )

    for copy in meta_copies:
        copy.wait_recv()
    row_meta = meta[0]
    for t in range(1, n_tp):
        row_meta = jnp.maximum(row_meta, meta[t])
    src_v[...] = row_meta
    to_scalar = pltpu.make_async_copy(src_v, src_s, local_sem.at[2])
    to_scalar.start()
    sl[0] = row_meta[2:3, :]
    sl_copies = [
        remote(sl.at[0], sl.at[k], sl_send.at[k], sl_recv.at[k], zc_dev(k)) for k in z_order
    ]
    code_column = jnp.concatenate(
        [
            jnp.transpose(jnp.broadcast_to(meta[t][0:1, :].astype(F32), (D, D)))[:tokens, :]
            for t in range(n_tp)
        ],
        axis=0,
    )
    allowed = code_column == row_code

    own_k.wait()
    for copy in k_copies:
        copy.wait_recv()
    for h in range(LOCAL_HEADS):
        dots = lax.dot_general(kp[:, pl.ds(h * D, D)], q_head(h), NT, preferred_element_type=F32)
        masked = jnp.where(allowed, dots * SCALE, NEGATIVE)
        scores[h] = masked
        mx[0, pl.ds(h, 1), :] = jnp.max(masked, axis=0, keepdims=True)
    mx_copies = [
        remote(mx.at[0], mx.at[k], mx_send.at[k], mx_recv.at[k], zc_dev(k)) for k in z_order
    ]

    def block_tile(ref, index):
        block = ref[index]
        return jnp.concatenate([block[:, :D], block[:, D:]], axis=0).astype(BF16)

    half = n_y // 2
    y_starts = [y_at(j) * n_zc for j in range(n_y)]
    zc_places = [zc_at(k) for k in range(n_zc)]

    def source_of(k, j):
        return src_s[1, y_starts[j] + zc_places[k]]

    def gather_z(x, staged, k):
        for i in range(half):
            tile = block_tile(staged, source_of(k, 2 * i))
            if k == 0:
                kb[x, 0, i] = tile
            else:
                ka[x, k, i] = tile

    def gather_y(x, staged, i):
        for k in range(n_zc):
            va[x, i, k] = block_tile(staged, source_of(k, 2 * i + 1))

    def z_first(x, k):
        return remote(ka.at[x, k], kb.at[x, k], z_send.at[x, 0, k], z_recv.at[x, 0, k], zc_dev(k))

    def y_first(x, i):
        return remote(
            va.at[x, i], vb.at[x, i], y_send.at[x, 0, i], y_recv.at[x, 0, i], y_dev(2 * i + 1)
        )

    def y_second(x, out, i):
        return remote(
            kb.at[x, :, i], out.at[0, i], y_send.at[x, 1, i], y_recv.at[x, 1, i], y_dev(2 * i)
        )

    def z_second(x, out, k):
        return remote(
            vb.at[x, :, k], out.at[1, :, k], z_send.at[x, 1, k], z_recv.at[x, 1, k], zc_dev(k)
        )

    local_copies = []

    def keep(src, dst):
        copy = pltpu.make_async_copy(src, dst, local_sem.at[3 + len(local_copies)])
        copy.start()
        local_copies.append(copy)

    k32[pl.ds(1, n_tp * own_blocks)] = kp[...].astype(F32).reshape(n_tp * own_blocks, TOK, PIECE)
    to_scalar.wait()

    kz1, ky1, vz1, vy1 = [], [], [], []
    per = -(-(n_zc - 1) // half)
    for n, i in enumerate(odd_order):
        gather_y(0, k32, i)
        ky1.append(y_first(0, i))
        for k in z_order[n * per : (n + 1) * per]:
            gather_z(0, k32, k)
            kz1.append(z_first(0, k))
    gather_z(0, k32, 0)

    own_v.wait()
    for copy in v_copies:
        copy.wait_recv()
    v32[pl.ds(1, n_tp * own_blocks)] = vp[...].astype(F32).reshape(n_tp * own_blocks, TOK, PIECE)
    for k in z_order:
        gather_z(1, v32, k)
        vz1.append(z_first(1, k))
    gather_z(1, v32, 0)
    for i in range(half):
        gather_y(1, v32, i)

    for copy in mx_copies:
        copy.wait_recv()
    row_max = mx[0]
    for k in range(1, n_zc):
        row_max = jnp.maximum(row_max, mx[k])
    my_buf[0] = row_max
    my_copies = [
        remote(my_buf.at[0], my_buf.at[j], my_send.at[j], my_recv.at[j], y_dev(j)) for j in y_order
    ]
    for copy in sl_copies:
        copy.wait_recv()
    for k in range(n_zc):
        sy[0, pl.ds(k, 1), :] = sl[k]
    sy_copies = [
        remote(sy.at[0], sy.at[j], sy_send.at[j], sy_recv.at[j], y_dev(j)) for j in y_order
    ]
    for i in odd_order:
        vy1.append(y_first(1, i))
    for copy in kz1:
        copy.wait_recv()
    ky2 = [y_second(0, kc, i) for i in even_order]
    keep(kb.at[0, :, 0], kc.at[0, 0])
    for copy in my_copies:
        copy.wait_recv()
    all_max = my_buf[0]
    for j in range(1, n_y):
        all_max = jnp.maximum(all_max, my_buf[j])

    chunk = D // n_zc
    row_tops = []
    for h in range(LOCAL_HEADS):
        row_top = jnp.maximum(
            all_max[h : h + 1, :], jnp.max(fresh_scores[h], axis=0, keepdims=True)
        )
        row_tops.append(row_top)
        weights = jnp.exp(scores[h] - row_top)
        su[mzc, pl.ds(h, 1), :] = jnp.sum(weights, axis=0, keepdims=True)
        number = lax.dot_general(
            vp[:, pl.ds(h * D, D)], weights.astype(BF16), TN, preferred_element_type=F32
        )
        for p in range(n_zc):
            rs_src[p, pl.ds(h * chunk, chunk), :] = number[p * chunk : (p + 1) * chunk, :]
    rs_copies = [
        remote(rs_src.at[zc_at(k)], rs_buf.at[mzc], rs_send.at[k], rs_recv.at[k], zc_dev(k))
        for k in z_order
    ]
    su_copies = [
        remote(su.at[mzc], su.at[mzc], su_send.at[k], su_recv.at[k], zc_dev(k)) for k in z_order
    ]
    rs_buf[mzc] = rs_src[mzc]

    for copy in ky1:
        copy.wait_recv()
    kz2 = [z_second(0, kc, k) for k in z_order]
    keep(vb.at[0, :, 0], kc.at[1, :, 0])

    fresh_totals = []
    for h in range(LOCAL_HEADS):
        weights = jnp.exp(fresh_scores[h] - row_tops[h])
        fresh_totals.append(jnp.sum(weights, axis=0, keepdims=True))
        number = lax.dot_general(
            fresh_vs[:, pl.ds(h * D, D)], weights.astype(BF16), TN, preferred_element_type=F32
        )
        for p in range(n_zc):
            fresh_num[p, pl.ds(h * chunk, chunk), :] = number[p * chunk : (p + 1) * chunk, :]

    for copy in sy_copies:
        copy.wait_recv()
    column = []
    for j in range(n_y):
        first_place = (j % 2) * half * n_zc + (j // 2) * n_zc + 1
        lists = sy[j]
        wide = lax.broadcasted_iota(jnp.int32, (n_zc, D), 1)
        picked = jnp.sum(jnp.where(wide == me, lists, 0), axis=1, keepdims=True)
        index = lax.broadcasted_iota(jnp.int32, (n_zc, D), 0) + first_place
        found = jnp.where(picked == wide + 1, index, 0)
        column.append(jnp.max(found, axis=0, keepdims=True))
    arrival = column[0]
    for j in range(1, n_y):
        arrival = jnp.maximum(arrival, column[j])
    arrival_ref[...] = jnp.broadcast_to(arrival, (8, D))

    for copy in rs_copies:
        copy.wait_recv()
    part = rs_buf[0]
    for p in range(1, n_zc):
        part = part + rs_buf[p]
    yy_buf[my] = part
    yy_copies = [
        remote(yy_buf.at[my], yy_buf.at[my], yy_send.at[j], yy_recv.at[j], y_dev(j)) for j in y_order
    ]
    for copy in su_copies:
        copy.wait_recv()
    part = su[0]
    for p in range(1, n_zc):
        part = part + su[p]
    sv[my] = part
    sv_copies = [
        remote(sv.at[my], sv.at[my], sv_send.at[j], sv_recv.at[j], y_dev(j)) for j in y_order
    ]

    for copy in vz1:
        copy.wait_recv()
    vy2 = [y_second(1, vc, i) for i in even_order]
    keep(kb.at[1, :, 0], vc.at[0, 0])
    for copy in vy1:
        copy.wait_recv()
    vz2 = [z_second(1, vc, k) for k in z_order[: n_zc // 2]]
    keep(vb.at[1, :, 0], vc.at[1, :, 0])

    for copy in yy_copies:
        copy.wait_recv()
    whole = yy_buf[0]
    for copy in sv_copies:
        copy.wait_recv()
    sums = sv[0]
    for j in range(1, n_y):
        whole = whole + yy_buf[j]
        sums = sums + sv[j]
    norms = []
    for h in range(LOCAL_HEADS):
        total = sums[h : h + 1, :] + fresh_totals[h]
        number = whole[h * chunk : (h + 1) * chunk, :] + fresh_num[mzc, pl.ds(h * chunk, chunk), :]
        ag_buf[mzc, pl.ds(h * chunk, chunk), :] = number / total
        norms.append(row_tops[h] + jnp.log(total))
    ag_copies = [
        remote(ag_buf.at[mzc], ag_buf.at[mzc], ag_send.at[k], ag_recv.at[k], zc_dev(k))
        for k in z_order
    ]
    vz2 += [z_second(1, vc, k) for k in z_order[n_zc // 2 :]]
    wide_lane = lax.broadcasted_iota(jnp.int32, (SR, D), 1)
    wide_row = lax.broadcasted_iota(jnp.int32, (SR, D), 0)
    by_head = jnp.zeros((SR, D), F32)
    for h in range(LOCAL_HEADS):
        for g in range(GROUP):
            picked = jnp.where(wide_lane == wide_row + g * SR, norms[h], 0.0)
            value = jnp.sum(picked, axis=1, keepdims=True)
            by_head = jnp.where(wide_lane == h * GROUP + g, value, by_head)
    norm_ref[...] = by_head
    for copy in ag_copies:
        copy.wait_recv()
    for h in range(LOCAL_HEADS):
        by_entry = jnp.concatenate(
            [ag_buf[p, pl.ds(h * chunk, chunk), :] for p in range(n_zc)], axis=0
        )
        by_row = jnp.transpose(by_entry)
        for g in range(GROUP):
            attended_ref[:, pl.ds((h * GROUP + g) * D, D)] = by_row[g * SR : (g + 1) * SR, :]

    for copy in kz2 + ky2 + vz2 + vy2:
        copy.wait_recv()
    for copy in local_copies:
        copy.wait()
    for copy in (
        meta_copies
        + k_copies
        + v_copies
        + sl_copies
        + sy_copies
        + su_copies
        + sv_copies
        + mx_copies
        + my_copies
        + kz1
        + ky1
        + kz2
        + ky2
        + vz1
        + vy1
        + vz2
        + vy2
        + rs_copies
        + yy_copies
        + ag_copies
    ):
        copy.wait_send()


def place_kernel(
    slot_count,
    arrival_ref,
    rows_ref,
    norm_ref,
    k_ref,
    v_ref,
    attended_ref,
    log_norm_ref,
    out_k_ref,
    out_v_ref,
):
    for s in range(STEPS):
        attended_ref[s] = rows_ref[pl.ds(s * REQUESTS, REQUESTS), :]
        log_norm_ref[s] = norm_ref[pl.ds(s * REQUESTS, REQUESTS), pl.ds(0, LOCAL_HEADS * GROUP)]

    def place(s, carry):
        index = arrival_ref[0, s]
        at = jnp.maximum(index - 1, 0)
        there = index > 0
        for ref, out in ((k_ref, out_k_ref), (v_ref, out_v_ref)):
            tile = ref[at].astype(F32)
            wide = jnp.concatenate([tile[:TOK, :], tile[TOK:, :]], axis=1)
            out[s] = jnp.where(there, wide, 0.0).astype(BF16)
        return carry

    lax.fori_loop(0, slot_count, place, 0, unroll=4)


def on_device(
    n_y,
    n_zc,
    prefilled_block_keys,
    prefilled_block_values,
    queries,
    step_token_keys,
    step_token_values,
    lengths,
    block_request,
    block_number,
    owner_rank,
    owner_slot,
    group_first,
):
    n_tp = lax.axis_size("tp")
    own_blocks, _, full_width = prefilled_block_keys.shape
    row_blocks = own_blocks * n_tp
    tokens = own_blocks * TOK
    slot_count = 2 * row_blocks
    n_sp = n_y * n_zc
    chunk = D // n_zc
    smem = pl.BlockSpec(memory_space=pltpu.SMEM)
    vmem = pl.BlockSpec(memory_space=pltpu.VMEM)
    hbm = pl.BlockSpec(memory_space=pltpu.HBM)
    half = n_y // 2
    dma = pltpu.SemaphoreType.DMA
    attended, norms, arrival, kc, vc = pl.pallas_call(
        functools.partial(exchange_kernel, n_y, n_zc, n_tp, own_blocks),
        out_shape=(
            jax.ShapeDtypeStruct((SR, GROUP * PIECE), F32),
            jax.ShapeDtypeStruct((SR, D), F32),
            jax.ShapeDtypeStruct((8, D), jnp.int32),
            jax.ShapeDtypeStruct((2, half, n_zc, 2 * TOK, D), BF16),
            jax.ShapeDtypeStruct((2, half, n_zc, 2 * TOK, D), BF16),
        ),
        in_specs=[smem] * 6 + [vmem] * 3 + [hbm] * 2,
        out_specs=(vmem,) * 5,
        scratch_shapes=[
            pltpu.VMEM((n_tp, 8, D), jnp.int32),
            pltpu.VMEM((n_tp * tokens, PIECE), BF16),
            pltpu.VMEM((n_tp * tokens, PIECE), BF16),
            pltpu.VMEM((row_blocks + 1, TOK, PIECE), F32),
            pltpu.VMEM((row_blocks + 1, TOK, PIECE), F32),
            pltpu.VMEM((8, D), jnp.int32),
            pltpu.SMEM((8, D), jnp.int32),
            pltpu.VMEM((LOCAL_HEADS, n_tp * tokens, ROWS), F32),
            pltpu.VMEM((2, n_zc, half, 2 * TOK, D), BF16),
            pltpu.VMEM((2, n_zc, half, 2 * TOK, D), BF16),
            pltpu.VMEM((2, half, n_zc, 2 * TOK, D), BF16),
            pltpu.VMEM((2, half, n_zc, 2 * TOK, D), BF16),
            pltpu.VMEM((SR, GROUP * PIECE), BF16),
            pltpu.VMEM((SR, PIECE), BF16),
            pltpu.VMEM((SR, PIECE), BF16),
            pltpu.VMEM((n_zc, 1, D), jnp.int32),
            pltpu.VMEM((n_y, n_zc, D), jnp.int32),
            pltpu.VMEM((n_zc, LOCAL_HEADS, ROWS), F32),
            pltpu.VMEM((n_y, LOCAL_HEADS, ROWS), F32),
            pltpu.VMEM((n_zc, LOCAL_HEADS, ROWS), F32),
            pltpu.VMEM((n_y, LOCAL_HEADS, ROWS), F32),
            pltpu.VMEM((n_zc, LOCAL_HEADS * chunk, ROWS), F32),
            pltpu.VMEM((n_zc, LOCAL_HEADS * chunk, ROWS), F32),
            pltpu.VMEM((n_zc, LOCAL_HEADS * chunk, ROWS), F32),
            pltpu.VMEM((n_y, LOCAL_HEADS * chunk, ROWS), F32),
            pltpu.VMEM((n_zc, LOCAL_HEADS * chunk, ROWS), F32),
            dma((7,)),
        ]
        + [dma((n_tp,))] * 6
        + [dma((n_zc,))] * 2
        + [dma((n_y,))] * 2
        + [dma((n_zc,))] * 2
        + [dma((n_y,))] * 2
        + [dma((n_zc,))] * 2
        + [dma((n_y,))] * 2
        + [dma((2, 2, n_zc))] * 2
        + [dma((2, 2, half))] * 2
        + [dma((n_zc,))] * 2
        + [dma((n_y,))] * 2
        + [dma((n_zc,))] * 2,
        compiler_params=pltpu.CompilerParams(
            collective_id=0, has_side_effects=True, vmem_limit_bytes=40 * 2**20
        ),
        name="exchange",
    )(
        block_request,
        block_number,
        owner_rank,
        owner_slot,
        lengths,
        group_first,
        queries,
        step_token_keys,
        step_token_values,
        pltpu.with_memory_space_constraint(prefilled_block_keys.reshape(tokens, full_width), pltpu.HBM),
        pltpu.with_memory_space_constraint(prefilled_block_values.reshape(tokens, full_width), pltpu.HBM),
    )
    slot_shape = jax.ShapeDtypeStruct((slot_count, TOK, PIECE), BF16)
    return pl.pallas_call(
        functools.partial(place_kernel, slot_count),
        out_shape=(
            jax.ShapeDtypeStruct((STEPS, REQUESTS, GROUP * PIECE), F32),
            jax.ShapeDtypeStruct((STEPS, REQUESTS, LOCAL_HEADS * GROUP), F32),
            slot_shape,
            slot_shape,
        ),
        in_specs=[smem] + [vmem] * 4,
        out_specs=(vmem,) * 4,
        compiler_params=pltpu.CompilerParams(vmem_limit_bytes=16 * 2**20),
        name="place",
    )(
        arrival,
        attended,
        norms,
        kc.reshape(n_sp, 2 * TOK, D),
        vc.reshape(n_sp, 2 * TOK, D),
    )


def solution(mesh):
    sp = mesh.shape["sp"]
    n_y = max(2, sp // 16)
    return jax.shard_map(
        functools.partial(on_device, n_y, sp // n_y),
        mesh=mesh,
        in_specs=(
            P(("sp", "tp"), None, None),
            P(("sp", "tp"), None, None),
            P(None, None, "tp"),
            P(None, None, "tp"),
            P(None, None, "tp"),
            P(),
            P(("sp", "tp")),
            P(("sp", "tp")),
            P(("sp", "tp")),
            P(("sp", "tp")),
            P(),
        ),
        out_specs=(
            P(None, None, "tp"),
            P(None, None, "tp"),
            P("sp", None, "tp"),
            P("sp", None, "tp"),
        ),
        check_vma=False,
    )
```

```python
import functools
import math

import jax
import jax.numpy as jnp
from jax import lax
from jax.experimental import pallas as pl
from jax.experimental.pallas import tpu as pltpu
from jax.sharding import PartitionSpec as P

D = 128
TOK = 8
STEPS = 4
REQUESTS = 4
SR = STEPS * REQUESTS
GROUP = 8
ROWS = GROUP * SR
LOCAL_HEADS = 2
PIECE = LOCAL_HEADS * D
NEGATIVE = -1e30
SCALE = 1.0 / math.sqrt(D)
MESH = pl.DeviceIdType.MESH
F32 = jnp.float32
BF16 = jnp.bfloat16
NT = (((1,), (1,)), ((), ()))
TN = (((0,), (0,)), ((), ()))


def exchange_kernel(
    n_y,
    n_zc,
    n_tp,
    own_blocks,
    request_hbm,
    number_hbm,
    rank_hbm,
    slot_hbm,
    lengths_hbm,
    first_hbm,
    q_hbm,
    fresh_k_hbm,
    fresh_v_hbm,
    keys_ref,
    values_ref,
    attended_ref,
    norm_ref,
    arrival_ref,
    kc,
    vc,
    meta,
    kp,
    vp,
    k32,
    v32,
    src_v,
    src_s,
    scores,
    ka,
    kb,
    va,
    vb,
    request_ref,
    number_ref,
    rank_ref,
    slot_ref,
    lengths_ref,
    first_ref,
    q_ref,
    fresh_k_ref,
    fresh_v_ref,
    operand_sem,
    qs,
    fresh_ks,
    fresh_vs,
    sl,
    sy,
    su,
    sv,
    mx,
    my_buf,
    fresh_num,
    rs_src,
    rs_buf,
    yy_buf,
    ag_buf,
    local_sem,
    meta_send,
    meta_recv,
    kp_send,
    kp_recv,
    vp_send,
    vp_recv,
    sl_send,
    sl_recv,
    sy_send,
    sy_recv,
    su_send,
    su_recv,
    sv_send,
    sv_recv,
    mx_send,
    mx_recv,
    my_send,
    my_recv,
    z_send,
    z_recv,
    y_send,
    y_recv,
    rs_send,
    rs_recv,
    yy_send,
    yy_recv,
    ag_send,
    ag_recv,
):
    me = lax.axis_index("sp")
    tp = lax.axis_index("tp")
    my = me // n_zc
    mzc = lax.rem(me, n_zc)
    tokens = own_blocks * TOK

    def zc_at(k):
        return lax.rem(mzc + k, n_zc)

    def y_at(j):
        return lax.rem(my + j, n_y)

    def tp_at(k):
        return lax.rem(tp + k, n_tp)

    z_order = sorted(range(1, n_zc), key=lambda k: -min(k, n_zc - k))
    y_order = sorted(range(1, n_y), key=lambda j: -min(j, n_y - j))
    odd_order = [(j - 1) // 2 for j in y_order if j % 2]
    even_order = [j // 2 for j in y_order if j % 2 == 0]

    def zc_dev(k):
        return (my * n_zc + zc_at(k), tp)

    def y_dev(j):
        return (y_at(j) * n_zc + mzc, tp)

    def tp_dev(k):
        return (me, tp_at(k))

    def remote(src, dst, send, recv, dev):
        copy = pltpu.make_async_remote_copy(
            src_ref=src, dst_ref=dst, send_sem=send, recv_sem=recv, device_id=dev, device_id_type=MESH
        )
        copy.start()
        return copy

    barrier = pltpu.get_barrier_semaphore()
    distant = [(min(k, n_zc - k) // 2, zc_dev(k)) for k in z_order]
    distant += [(min(j, n_y - j), y_dev(j)) for j in y_order]
    distant += [(min(k, n_tp - k), tp_dev(k)) for k in range(1, n_tp)]
    peers = [dev for _, dev in sorted(distant, key=lambda pair: -pair[0])]
    for dev in peers:
        pl.semaphore_signal(barrier, inc=1, device_id=dev, device_id_type=MESH)

    def columns(t):
        return pl.ds(pl.multiple_of(t * PIECE, PIECE), PIECE)

    def rows_of(t):
        return pl.ds(pl.multiple_of(t * tokens, tokens), tokens)

    own_k = pltpu.make_async_copy(keys_ref.at[:, columns(tp)], kp.at[rows_of(tp)], local_sem.at[0])
    own_v = pltpu.make_async_copy(values_ref.at[:, columns(tp)], vp.at[rows_of(tp)], local_sem.at[1])
    own_k.start()
    own_v.start()

    fetches = [
        pltpu.make_async_copy(src, dst, operand_sem.at[n])
        for n, (src, dst) in enumerate(
            (
                (request_hbm, request_ref),
                (number_hbm, number_ref),
                (rank_hbm, rank_ref),
                (slot_hbm, slot_ref),
                (lengths_hbm, lengths_ref),
                (first_hbm, first_ref),
                (q_hbm, q_ref),
                (fresh_k_hbm, fresh_k_ref),
                (fresh_v_hbm, fresh_v_ref),
            )
        )
    ]
    for fetch in fetches:
        fetch.start()
    for fetch in fetches:
        fetch.wait()

    lane = lax.broadcasted_iota(jnp.int32, (1, D), 1)
    codes = jnp.full((1, D), REQUESTS, jnp.int32)
    sources = jnp.zeros((1, D), jnp.int32)
    slots = jnp.zeros((1, D), jnp.int32)
    for b in range(own_blocks):
        request = request_ref[b]
        owner = first_ref[request] + rank_ref[b]
        place = number_ref[b] * TOK + (lane - b * TOK)
        mine = (lane >= b * TOK) & (lane < (b + 1) * TOK) & (place < lengths_ref[request])
        codes = jnp.where(mine, request, codes)
        hit = lane == owner
        sources = jnp.where(hit, tp * own_blocks + b + 1, sources)
        slots = jnp.where(hit, slot_ref[b] + 1, slots)
    own_meta = jnp.concatenate(
        [codes, sources, slots, jnp.zeros((5, D), jnp.int32)], axis=0
    )
    meta[tp] = own_meta

    row_lane = lax.broadcasted_iota(jnp.int32, (1, ROWS), 1)
    row_request = lax.rem(row_lane, REQUESTS)
    row_step = lax.rem(row_lane, SR) // REQUESTS
    row_code = row_request.astype(F32)

    def stack_steps(ref, out):
        out[...] = jnp.concatenate([ref[s].astype(F32) for s in range(STEPS)], axis=0).astype(BF16)

    stack_steps(q_ref, qs)
    stack_steps(fresh_k_ref, fresh_ks)
    stack_steps(fresh_v_ref, fresh_vs)

    def q_head(h):
        return jnp.concatenate(
            [qs[:, pl.ds((h * GROUP + g) * D, D)] for g in range(GROUP)], axis=0
        )

    fresh_row = lax.broadcasted_iota(jnp.int32, (SR, ROWS), 0)
    fresh_ok = (lax.rem(fresh_row, REQUESTS) == row_request) & (fresh_row // REQUESTS <= row_step)
    fresh_scores = []
    for h in range(LOCAL_HEADS):
        dots = lax.dot_general(
            fresh_ks[:, pl.ds(h * D, D)], q_head(h), NT, preferred_element_type=F32
        )
        fresh_scores.append(jnp.where(fresh_ok, dots * SCALE, NEGATIVE))

    k32[0] = jnp.zeros((TOK, PIECE), F32)
    v32[0] = jnp.zeros((TOK, PIECE), F32)

    pl.semaphore_wait(barrier, len(peers))

    meta_copies, k_copies, v_copies = [], [], []
    for k in range(1, n_tp):
        meta_copies.append(
            remote(meta.at[tp], meta.at[tp], meta_send.at[k], meta_recv.at[k], tp_dev(k))
        )
    for k in range(1, n_tp):
        k_copies.append(
            remote(keys_ref.at[:, columns(tp_at(k))], kp.at[rows_of(tp)], kp_send.at[k], kp_recv.at[k], tp_dev(k))
        )
    for k in range(1, n_tp):
        v_copies.append(
            remote(
                values_ref.at[:, columns(tp_at(k))], vp.at[rows_of(tp)], vp_send.at[k], vp_recv.at[k], tp_dev(k)
            )
        )

    for copy in meta_copies:
        copy.wait_recv()
    row_meta = meta[0]
    for t in range(1, n_tp):
        row_meta = jnp.maximum(row_meta, meta[t])
    src_v[...] = row_meta
    to_scalar = pltpu.make_async_copy(src_v, src_s, local_sem.at[2])
    to_scalar.start()
    sl[0] = row_meta[2:3, :]
    sl_copies = [
        remote(sl.at[0], sl.at[k], sl_send.at[k], sl_recv.at[k], zc_dev(k)) for k in z_order
    ]
    code_column = jnp.concatenate(
        [
            jnp.transpose(jnp.broadcast_to(meta[t][0:1, :].astype(F32), (D, D)))[:tokens, :]
            for t in range(n_tp)
        ],
        axis=0,
    )
    allowed = code_column == row_code

    own_k.wait()
    for copy in k_copies:
        copy.wait_recv()
    for h in range(LOCAL_HEADS):
        dots = lax.dot_general(kp[:, pl.ds(h * D, D)], q_head(h), NT, preferred_element_type=F32)
        masked = jnp.where(allowed, dots * SCALE, NEGATIVE)
        scores[h] = masked
        mx[0, pl.ds(h, 1), :] = jnp.max(masked, axis=0, keepdims=True)
    mx_copies = [
        remote(mx.at[0], mx.at[k], mx_send.at[k], mx_recv.at[k], zc_dev(k)) for k in z_order
    ]

    def block_tile(ref, index):
        block = ref[index]
        return jnp.concatenate([block[:, :D], block[:, D:]], axis=0).astype(BF16)

    half = n_y // 2
    y_starts = [y_at(j) * n_zc for j in range(n_y)]

    def source_of(k, j):
        return src_s[1, y_starts[j] + zc_at(k)]

    def gather_z(x, staged, k):
        for i in range(half):
            tile = block_tile(staged, source_of(k, 2 * i))
            if isinstance(k, int):
                kb[x, 0, i] = tile
            else:
                ka[x, k, i] = tile

    def gather_y(x, staged, i):
        def step(k, carry):
            va[x, i, k] = block_tile(staged, source_of(k, 2 * i + 1))
            return carry

        lax.fori_loop(0, n_zc, step, 0, unroll=4)

    def z_sends(x, staged, first, last):
        def step(n, carry):
            away = (n + 1) // 2
            k = n_zc // 2 + jnp.where(lax.rem(n, 2) == 1, away, -away)
            gather_z(x, staged, k)
            z_first(x, k).start()
            return carry

        lax.fori_loop(first, last, step, 0)

    def z_first(x, k):
        return pltpu.make_async_remote_copy(
            src_ref=ka.at[x, k],
            dst_ref=kb.at[x, k],
            send_sem=z_send.at[x, 0, k],
            recv_sem=z_recv.at[x, 0, k],
            device_id=zc_dev(k),
            device_id_type=MESH,
        )

    def y_first(x, i):
        return remote(
            va.at[x, i], vb.at[x, i], y_send.at[x, 0, i], y_recv.at[x, 0, i], y_dev(2 * i + 1)
        )

    def y_second(x, out, i):
        return remote(
            kb.at[x, :, i], out.at[0, i], y_send.at[x, 1, i], y_recv.at[x, 1, i], y_dev(2 * i)
        )

    def z_second(x, out, k):
        return remote(
            vb.at[x, :, k], out.at[1, :, k], z_send.at[x, 1, k], z_recv.at[x, 1, k], zc_dev(k)
        )

    local_copies = []

    def keep(src, dst):
        copy = pltpu.make_async_copy(src, dst, local_sem.at[3 + len(local_copies)])
        copy.start()
        local_copies.append(copy)

    k32[pl.ds(1, n_tp * own_blocks)] = kp[...].astype(F32).reshape(n_tp * own_blocks, TOK, PIECE)
    to_scalar.wait()

    ky1, vy1 = [], []
    kz1 = [z_first(0, k) for k in range(1, n_zc)]
    vz1 = [z_first(1, k) for k in range(1, n_zc)]
    per = -(-(n_zc - 1) // half)
    for n, i in enumerate(odd_order):
        gather_y(0, k32, i)
        ky1.append(y_first(0, i))
        z_sends(0, k32, n * per, min(n_zc - 1, (n + 1) * per))
    gather_z(0, k32, 0)

    own_v.wait()
    for copy in v_copies:
        copy.wait_recv()
    v32[pl.ds(1, n_tp * own_blocks)] = vp[...].astype(F32).reshape(n_tp * own_blocks, TOK, PIECE)
    z_sends(1, v32, 0, n_zc - 1)
    gather_z(1, v32, 0)
    for i in range(half):
        gather_y(1, v32, i)

    for copy in mx_copies:
        copy.wait_recv()
    row_max = mx[0]
    for k in range(1, n_zc):
        row_max = jnp.maximum(row_max, mx[k])
    my_buf[0] = row_max
    my_copies = [
        remote(my_buf.at[0], my_buf.at[j], my_send.at[j], my_recv.at[j], y_dev(j)) for j in y_order
    ]
    for copy in sl_copies:
        copy.wait_recv()
    for k in range(n_zc):
        sy[0, pl.ds(k, 1), :] = sl[k]
    sy_copies = [
        remote(sy.at[0], sy.at[j], sy_send.at[j], sy_recv.at[j], y_dev(j)) for j in y_order
    ]
    for i in odd_order:
        vy1.append(y_first(1, i))
    for copy in kz1:
        copy.wait_recv()
    ky2 = [y_second(0, kc, i) for i in even_order]
    keep(kb.at[0, :, 0], kc.at[0, 0])
    for copy in my_copies:
        copy.wait_recv()
    all_max = my_buf[0]
    for j in range(1, n_y):
        all_max = jnp.maximum(all_max, my_buf[j])

    chunk = D // n_zc
    row_tops = []
    for h in range(LOCAL_HEADS):
        row_top = jnp.maximum(
            all_max[h : h + 1, :], jnp.max(fresh_scores[h], axis=0, keepdims=True)
        )
        row_tops.append(row_top)
        weights = jnp.exp(scores[h] - row_top)
        su[mzc, pl.ds(h, 1), :] = jnp.sum(weights, axis=0, keepdims=True)
        number = lax.dot_general(
            vp[:, pl.ds(h * D, D)], weights.astype(BF16), TN, preferred_element_type=F32
        )
        for p in range(n_zc):
            rs_src[p, pl.ds(h * chunk, chunk), :] = number[p * chunk : (p + 1) * chunk, :]
    rs_copies = [
        remote(rs_src.at[zc_at(k)], rs_buf.at[mzc], rs_send.at[k], rs_recv.at[k], zc_dev(k))
        for k in z_order
    ]
    su_copies = [
        remote(su.at[mzc], su.at[mzc], su_send.at[k], su_recv.at[k], zc_dev(k)) for k in z_order
    ]
    rs_buf[mzc] = rs_src[mzc]

    for copy in ky1:
        copy.wait_recv()
    kz2 = [z_second(0, kc, k) for k in z_order]
    keep(vb.at[0, :, 0], kc.at[1, :, 0])

    fresh_totals = []
    for h in range(LOCAL_HEADS):
        weights = jnp.exp(fresh_scores[h] - row_tops[h])
        fresh_totals.append(jnp.sum(weights, axis=0, keepdims=True))
        number = lax.dot_general(
            fresh_vs[:, pl.ds(h * D, D)], weights.astype(BF16), TN, preferred_element_type=F32
        )
        for p in range(n_zc):
            fresh_num[p, pl.ds(h * chunk, chunk), :] = number[p * chunk : (p + 1) * chunk, :]

    for copy in sy_copies:
        copy.wait_recv()
    column = []
    for j in range(n_y):
        first_place = (j % 2) * half * n_zc + (j // 2) * n_zc + 1
        lists = sy[j]
        wide = lax.broadcasted_iota(jnp.int32, (n_zc, D), 1)
        picked = jnp.sum(jnp.where(wide == me, lists, 0), axis=1, keepdims=True)
        index = lax.broadcasted_iota(jnp.int32, (n_zc, D), 0) + first_place
        found = jnp.where(picked == wide + 1, index, 0)
        column.append(jnp.max(found, axis=0, keepdims=True))
    arrival = column[0]
    for j in range(1, n_y):
        arrival = jnp.maximum(arrival, column[j])
    arrival_ref[...] = jnp.broadcast_to(arrival, (8, D))

    for copy in rs_copies:
        copy.wait_recv()
    part = rs_buf[0]
    for p in range(1, n_zc):
        part = part + rs_buf[p]
    yy_buf[my] = part
    yy_copies = [
        remote(yy_buf.at[my], yy_buf.at[my], yy_send.at[j], yy_recv.at[j], y_dev(j)) for j in y_order
    ]
    for copy in su_copies:
        copy.wait_recv()
    part = su[0]
    for p in range(1, n_zc):
        part = part + su[p]
    sv[my] = part
    sv_copies = [
        remote(sv.at[my], sv.at[my], sv_send.at[j], sv_recv.at[j], y_dev(j)) for j in y_order
    ]

    for copy in vz1:
        copy.wait_recv()
    vy2 = [y_second(1, vc, i) for i in even_order]
    keep(kb.at[1, :, 0], vc.at[0, 0])
    for copy in vy1:
        copy.wait_recv()
    vz2 = [z_second(1, vc, k) for k in z_order[: n_zc // 2]]
    keep(vb.at[1, :, 0], vc.at[1, :, 0])

    for copy in yy_copies:
        copy.wait_recv()
    whole = yy_buf[0]
    for copy in sv_copies:
        copy.wait_recv()
    sums = sv[0]
    for j in range(1, n_y):
        whole = whole + yy_buf[j]
        sums = sums + sv[j]
    norms = []
    for h in range(LOCAL_HEADS):
        total = sums[h : h + 1, :] + fresh_totals[h]
        number = whole[h * chunk : (h + 1) * chunk, :] + fresh_num[mzc, pl.ds(h * chunk, chunk), :]
        ag_buf[mzc, pl.ds(h * chunk, chunk), :] = number / total
        norms.append(row_tops[h] + jnp.log(total))
    ag_copies = [
        remote(ag_buf.at[mzc], ag_buf.at[mzc], ag_send.at[k], ag_recv.at[k], zc_dev(k))
        for k in z_order
    ]
    vz2 += [z_second(1, vc, k) for k in z_order[n_zc // 2 :]]
    wide_lane = lax.broadcasted_iota(jnp.int32, (SR, D), 1)
    wide_row = lax.broadcasted_iota(jnp.int32, (SR, D), 0)
    by_head = jnp.zeros((SR, D), F32)
    for h in range(LOCAL_HEADS):
        for g in range(GROUP):
            picked = jnp.where(wide_lane == wide_row + g * SR, norms[h], 0.0)
            value = jnp.sum(picked, axis=1, keepdims=True)
            by_head = jnp.where(wide_lane == h * GROUP + g, value, by_head)
    norm_ref[...] = by_head
    for copy in ag_copies:
        copy.wait_recv()
    for h in range(LOCAL_HEADS):
        by_entry = jnp.concatenate(
            [ag_buf[p, pl.ds(h * chunk, chunk), :] for p in range(n_zc)], axis=0
        )
        by_row = jnp.transpose(by_entry)
        for g in range(GROUP):
            attended_ref[:, pl.ds((h * GROUP + g) * D, D)] = by_row[g * SR : (g + 1) * SR, :]

    for copy in kz2 + ky2 + vz2 + vy2:
        copy.wait_recv()
    for copy in local_copies:
        copy.wait()
    for copy in (
        meta_copies
        + k_copies
        + v_copies
        + sl_copies
        + sy_copies
        + su_copies
        + sv_copies
        + mx_copies
        + my_copies
        + kz1
        + ky1
        + kz2
        + ky2
        + vz1
        + vy1
        + vz2
        + vy2
        + rs_copies
        + yy_copies
        + ag_copies
    ):
        copy.wait_send()


def place_kernel(
    slot_count,
    arrival_ref,
    rows_ref,
    norm_ref,
    k_ref,
    v_ref,
    attended_ref,
    log_norm_ref,
    out_k_ref,
    out_v_ref,
):
    for s in range(STEPS):
        attended_ref[s] = rows_ref[pl.ds(s * REQUESTS, REQUESTS), :]
        log_norm_ref[s] = norm_ref[pl.ds(s * REQUESTS, REQUESTS), pl.ds(0, LOCAL_HEADS * GROUP)]

    def place(s, carry):
        index = arrival_ref[0, s]
        at = jnp.maximum(index - 1, 0)
        there = index > 0
        for ref, out in ((k_ref, out_k_ref), (v_ref, out_v_ref)):
            tile = ref[at].astype(F32)
            wide = jnp.concatenate([tile[:TOK, :], tile[TOK:, :]], axis=1)
            out[s] = jnp.where(there, wide, 0.0).astype(BF16)
        return carry

    lax.fori_loop(0, slot_count, place, 0, unroll=4)


def on_device(
    n_y,
    n_zc,
    prefilled_block_keys,
    prefilled_block_values,
    queries,
    step_token_keys,
    step_token_values,
    lengths,
    block_request,
    block_number,
    owner_rank,
    owner_slot,
    group_first,
):
    n_tp = lax.axis_size("tp")
    own_blocks, _, full_width = prefilled_block_keys.shape
    row_blocks = own_blocks * n_tp
    tokens = own_blocks * TOK
    slot_count = 2 * row_blocks
    n_sp = n_y * n_zc
    chunk = D // n_zc
    smem = pl.BlockSpec(memory_space=pltpu.SMEM)
    vmem = pl.BlockSpec(memory_space=pltpu.VMEM)
    hbm = pl.BlockSpec(memory_space=pltpu.HBM)
    half = n_y // 2
    dma = pltpu.SemaphoreType.DMA
    attended, norms, arrival, kc, vc = pl.pallas_call(
        functools.partial(exchange_kernel, n_y, n_zc, n_tp, own_blocks),
        out_shape=(
            jax.ShapeDtypeStruct((SR, GROUP * PIECE), F32),
            jax.ShapeDtypeStruct((SR, D), F32),
            jax.ShapeDtypeStruct((8, D), jnp.int32),
            jax.ShapeDtypeStruct((2, half, n_zc, 2 * TOK, D), BF16),
            jax.ShapeDtypeStruct((2, half, n_zc, 2 * TOK, D), BF16),
        ),
        in_specs=[hbm] * 11,
        out_specs=(vmem,) * 5,
        scratch_shapes=[
            pltpu.VMEM((n_tp, 8, D), jnp.int32),
            pltpu.VMEM((n_tp * tokens, PIECE), BF16),
            pltpu.VMEM((n_tp * tokens, PIECE), BF16),
            pltpu.VMEM((row_blocks + 1, TOK, PIECE), F32),
            pltpu.VMEM((row_blocks + 1, TOK, PIECE), F32),
            pltpu.VMEM((8, D), jnp.int32),
            pltpu.SMEM((8, D), jnp.int32),
            pltpu.VMEM((LOCAL_HEADS, n_tp * tokens, ROWS), F32),
            pltpu.VMEM((2, n_zc, half, 2 * TOK, D), BF16),
            pltpu.VMEM((2, n_zc, half, 2 * TOK, D), BF16),
            pltpu.VMEM((2, half, n_zc, 2 * TOK, D), BF16),
            pltpu.VMEM((2, half, n_zc, 2 * TOK, D), BF16),
            pltpu.SMEM((own_blocks,), jnp.int32),
            pltpu.SMEM((own_blocks,), jnp.int32),
            pltpu.SMEM((own_blocks,), jnp.int32),
            pltpu.SMEM((own_blocks,), jnp.int32),
            pltpu.SMEM((REQUESTS,), jnp.int32),
            pltpu.SMEM((REQUESTS,), jnp.int32),
            pltpu.VMEM((STEPS, REQUESTS, GROUP * PIECE), BF16),
            pltpu.VMEM((STEPS, REQUESTS, PIECE), BF16),
            pltpu.VMEM((STEPS, REQUESTS, PIECE), BF16),
            dma((9,)),
            pltpu.VMEM((SR, GROUP * PIECE), BF16),
            pltpu.VMEM((SR, PIECE), BF16),
            pltpu.VMEM((SR, PIECE), BF16),
            pltpu.VMEM((n_zc, 1, D), jnp.int32),
            pltpu.VMEM((n_y, n_zc, D), jnp.int32),
            pltpu.VMEM((n_zc, LOCAL_HEADS, ROWS), F32),
            pltpu.VMEM((n_y, LOCAL_HEADS, ROWS), F32),
            pltpu.VMEM((n_zc, LOCAL_HEADS, ROWS), F32),
            pltpu.VMEM((n_y, LOCAL_HEADS, ROWS), F32),
            pltpu.VMEM((n_zc, LOCAL_HEADS * chunk, ROWS), F32),
            pltpu.VMEM((n_zc, LOCAL_HEADS * chunk, ROWS), F32),
            pltpu.VMEM((n_zc, LOCAL_HEADS * chunk, ROWS), F32),
            pltpu.VMEM((n_y, LOCAL_HEADS * chunk, ROWS), F32),
            pltpu.VMEM((n_zc, LOCAL_HEADS * chunk, ROWS), F32),
            dma((7,)),
        ]
        + [dma((n_tp,))] * 6
        + [dma((n_zc,))] * 2
        + [dma((n_y,))] * 2
        + [dma((n_zc,))] * 2
        + [dma((n_y,))] * 2
        + [dma((n_zc,))] * 2
        + [dma((n_y,))] * 2
        + [dma((2, 2, n_zc))] * 2
        + [dma((2, 2, half))] * 2
        + [dma((n_zc,))] * 2
        + [dma((n_y,))] * 2
        + [dma((n_zc,))] * 2,
        compiler_params=pltpu.CompilerParams(
            collective_id=0, has_side_effects=True, vmem_limit_bytes=40 * 2**20
        ),
        name="exchange",
    )(
        *[
            pltpu.with_memory_space_constraint(operand, pltpu.HBM)
            for operand in (
                block_request,
                block_number,
                owner_rank,
                owner_slot,
                lengths,
                group_first,
                queries,
                step_token_keys,
                step_token_values,
                prefilled_block_keys.reshape(tokens, full_width),
                prefilled_block_values.reshape(tokens, full_width),
            )
        ]
    )
    slot_shape = jax.ShapeDtypeStruct((slot_count, TOK, PIECE), BF16)
    return pl.pallas_call(
        functools.partial(place_kernel, slot_count),
        out_shape=(
            jax.ShapeDtypeStruct((STEPS, REQUESTS, GROUP * PIECE), F32),
            jax.ShapeDtypeStruct((STEPS, REQUESTS, LOCAL_HEADS * GROUP), F32),
            slot_shape,
            slot_shape,
        ),
        in_specs=[smem] + [vmem] * 4,
        out_specs=(vmem,) * 4,
        compiler_params=pltpu.CompilerParams(vmem_limit_bytes=16 * 2**20),
        name="place",
    )(
        arrival,
        attended,
        norms,
        kc.reshape(n_sp, 2 * TOK, D),
        vc.reshape(n_sp, 2 * TOK, D),
    )


def solution(mesh):
    sp = mesh.shape["sp"]
    n_y = max(2, sp // 16)
    return jax.shard_map(
        functools.partial(on_device, n_y, sp // n_y),
        mesh=mesh,
        in_specs=(
            P(("sp", "tp"), None, None),
            P(("sp", "tp"), None, None),
            P(None, None, "tp"),
            P(None, None, "tp"),
            P(None, None, "tp"),
            P(),
            P(("sp", "tp")),
            P(("sp", "tp")),
            P(("sp", "tp")),
            P(("sp", "tp")),
            P(),
        ),
        out_specs=(
            P(None, None, "tp"),
            P(None, None, "tp"),
            P("sp", None, "tp"),
            P("sp", None, "tp"),
        ),
        check_vma=False,
    )
```

```python
import functools
import math

import jax
import jax.numpy as jnp
from jax import lax
from jax.experimental import pallas as pl
from jax.experimental.pallas import tpu as pltpu
from jax.sharding import PartitionSpec as P

D = 128
TOK = 8
STEPS = 4
REQUESTS = 4
SR = STEPS * REQUESTS
GROUP = 8
ROWS = GROUP * SR
LOCAL_HEADS = 2
PIECE = LOCAL_HEADS * D
NEGATIVE = -1e30
SCALE = 1.0 / math.sqrt(D)
MESH = pl.DeviceIdType.MESH
F32 = jnp.float32
BF16 = jnp.bfloat16
NT = (((1,), (1,)), ((), ()))
TN = (((0,), (0,)), ((), ()))


def exchange_kernel(
    n_y,
    n_zc,
    n_tp,
    own_blocks,
    request_hbm,
    number_hbm,
    rank_hbm,
    slot_hbm,
    lengths_hbm,
    first_hbm,
    q_hbm,
    fresh_k_hbm,
    fresh_v_hbm,
    keys_ref,
    values_ref,
    attended_ref,
    norm_ref,
    arrival_ref,
    kc,
    vc,
    meta,
    kp,
    vp,
    k32,
    v32,
    src_v,
    src_s,
    scores,
    ka,
    kb,
    va,
    vb,
    request_ref,
    number_ref,
    rank_ref,
    slot_ref,
    lengths_ref,
    first_ref,
    q_ref,
    fresh_k_ref,
    fresh_v_ref,
    operand_sem,
    qs,
    fresh_ks,
    fresh_vs,
    sl,
    sy,
    su,
    sv,
    mx,
    my_buf,
    fresh_num,
    rs_src,
    rs_buf,
    yy_buf,
    ag_buf,
    local_sem,
    meta_send,
    meta_recv,
    kp_send,
    kp_recv,
    vp_send,
    vp_recv,
    sl_send,
    sl_recv,
    sy_send,
    sy_recv,
    su_send,
    su_recv,
    sv_send,
    sv_recv,
    mx_send,
    mx_recv,
    my_send,
    my_recv,
    z_send,
    z_recv,
    y_send,
    y_recv,
    rs_send,
    rs_recv,
    yy_send,
    yy_recv,
    ag_send,
    ag_recv,
):
    me = lax.axis_index("sp")
    tp = lax.axis_index("tp")
    my = me // n_zc
    mzc = lax.rem(me, n_zc)
    tokens = own_blocks * TOK

    def zc_at(k):
        return lax.rem(mzc + k, n_zc)

    def y_at(j):
        return lax.rem(my + j, n_y)

    def tp_at(k):
        return lax.rem(tp + k, n_tp)

    z_order = sorted(range(1, n_zc), key=lambda k: -min(k, n_zc - k))
    y_order = sorted(range(1, n_y), key=lambda j: -min(j, n_y - j))
    odd_order = [(j - 1) // 2 for j in y_order if j % 2]
    even_order = [j // 2 for j in y_order if j % 2 == 0]

    def zc_dev(k):
        return (my * n_zc + zc_at(k), tp)

    def y_dev(j):
        return (y_at(j) * n_zc + mzc, tp)

    def tp_dev(k):
        return (me, tp_at(k))

    def remote(src, dst, send, recv, dev):
        copy = pltpu.make_async_remote_copy(
            src_ref=src, dst_ref=dst, send_sem=send, recv_sem=recv, device_id=dev, device_id_type=MESH
        )
        copy.start()
        return copy

    barrier = pltpu.get_barrier_semaphore()
    distant = [(min(k, n_zc - k) // 2, zc_dev(k)) for k in z_order]
    distant += [(min(j, n_y - j), y_dev(j)) for j in y_order]
    distant += [(min(k, n_tp - k), tp_dev(k)) for k in range(1, n_tp)]
    peers = [dev for _, dev in sorted(distant, key=lambda pair: -pair[0])]
    for dev in peers:
        pl.semaphore_signal(barrier, inc=1, device_id=dev, device_id_type=MESH)

    def columns(t):
        return pl.ds(pl.multiple_of(t * PIECE, PIECE), PIECE)

    def rows_of(t):
        return pl.ds(pl.multiple_of(t * tokens, tokens), tokens)

    own_k = pltpu.make_async_copy(keys_ref.at[:, columns(tp)], kp.at[rows_of(tp)], local_sem.at[0])
    own_v = pltpu.make_async_copy(values_ref.at[:, columns(tp)], vp.at[rows_of(tp)], local_sem.at[1])
    own_k.start()
    own_v.start()

    fetches = [
        pltpu.make_async_copy(src, dst, operand_sem.at[n])
        for n, (src, dst) in enumerate(
            (
                (request_hbm, request_ref),
                (number_hbm, number_ref),
                (rank_hbm, rank_ref),
                (slot_hbm, slot_ref),
                (lengths_hbm, lengths_ref),
                (first_hbm, first_ref),
                (q_hbm, q_ref),
                (fresh_k_hbm, fresh_k_ref),
                (fresh_v_hbm, fresh_v_ref),
            )
        )
    ]
    for fetch in fetches:
        fetch.start()
    for fetch in fetches:
        fetch.wait()

    lane = lax.broadcasted_iota(jnp.int32, (1, D), 1)
    codes = jnp.full((1, D), REQUESTS, jnp.int32)
    sources = jnp.zeros((1, D), jnp.int32)
    slots = jnp.zeros((1, D), jnp.int32)
    for b in range(own_blocks):
        request = request_ref[b]
        owner = first_ref[request] + rank_ref[b]
        place = number_ref[b] * TOK + (lane - b * TOK)
        mine = (lane >= b * TOK) & (lane < (b + 1) * TOK) & (place < lengths_ref[request])
        codes = jnp.where(mine, request, codes)
        hit = lane == owner
        sources = jnp.where(hit, tp * own_blocks + b + 1, sources)
        slots = jnp.where(hit, slot_ref[b] + 1, slots)
    own_meta = jnp.concatenate(
        [codes, sources, slots, jnp.zeros((5, D), jnp.int32)], axis=0
    )
    meta[tp] = own_meta

    row_lane = lax.broadcasted_iota(jnp.int32, (1, ROWS), 1)
    row_request = lax.rem(row_lane, REQUESTS)
    row_step = lax.rem(row_lane, SR) // REQUESTS
    row_code = row_request.astype(F32)

    def stack_steps(ref, out):
        out[...] = jnp.concatenate([ref[s].astype(F32) for s in range(STEPS)], axis=0).astype(BF16)

    stack_steps(q_ref, qs)
    stack_steps(fresh_k_ref, fresh_ks)
    stack_steps(fresh_v_ref, fresh_vs)

    def q_head(h):
        return jnp.concatenate(
            [qs[:, pl.ds((h * GROUP + g) * D, D)] for g in range(GROUP)], axis=0
        )

    fresh_row = lax.broadcasted_iota(jnp.int32, (SR, ROWS), 0)
    fresh_ok = (lax.rem(fresh_row, REQUESTS) == row_request) & (fresh_row // REQUESTS <= row_step)
    fresh_scores = []
    for h in range(LOCAL_HEADS):
        dots = lax.dot_general(
            fresh_ks[:, pl.ds(h * D, D)], q_head(h), NT, preferred_element_type=F32
        )
        fresh_scores.append(jnp.where(fresh_ok, dots * SCALE, NEGATIVE))

    k32[0] = jnp.zeros((TOK, PIECE), F32)
    v32[0] = jnp.zeros((TOK, PIECE), F32)

    pl.semaphore_wait(barrier, len(peers))

    meta_copies, k_copies, v_copies = [], [], []
    for k in range(1, n_tp):
        meta_copies.append(
            remote(meta.at[tp], meta.at[tp], meta_send.at[k], meta_recv.at[k], tp_dev(k))
        )
    for k in range(1, n_tp):
        k_copies.append(
            remote(keys_ref.at[:, columns(tp_at(k))], kp.at[rows_of(tp)], kp_send.at[k], kp_recv.at[k], tp_dev(k))
        )
    for k in range(1, n_tp):
        v_copies.append(
            remote(
                values_ref.at[:, columns(tp_at(k))], vp.at[rows_of(tp)], vp_send.at[k], vp_recv.at[k], tp_dev(k)
            )
        )

    for copy in meta_copies:
        copy.wait_recv()
    row_meta = meta[0]
    for t in range(1, n_tp):
        row_meta = jnp.maximum(row_meta, meta[t])
    src_v[...] = row_meta
    to_scalar = pltpu.make_async_copy(src_v, src_s, local_sem.at[2])
    to_scalar.start()
    sl[0] = row_meta[2:3, :]
    sl_copies = [
        remote(sl.at[0], sl.at[k], sl_send.at[k], sl_recv.at[k], zc_dev(k)) for k in z_order
    ]
    code_column = jnp.concatenate(
        [
            jnp.transpose(jnp.broadcast_to(meta[t][0:1, :].astype(F32), (D, D)))[:tokens, :]
            for t in range(n_tp)
        ],
        axis=0,
    )
    allowed = code_column == row_code

    own_k.wait()
    for copy in k_copies:
        copy.wait_recv()
    for h in range(LOCAL_HEADS):
        dots = lax.dot_general(kp[:, pl.ds(h * D, D)], q_head(h), NT, preferred_element_type=F32)
        masked = jnp.where(allowed, dots * SCALE, NEGATIVE)
        scores[h] = masked
        mx[0, pl.ds(h, 1), :] = jnp.max(masked, axis=0, keepdims=True)
    mx_copies = [
        remote(mx.at[0], mx.at[k], mx_send.at[k], mx_recv.at[k], zc_dev(k)) for k in z_order
    ]

    def block_tile(ref, index):
        block = ref[index]
        return jnp.concatenate([block[:, :D], block[:, D:]], axis=0).astype(BF16)

    half = n_y // 2
    y_starts = [y_at(j) * n_zc for j in range(n_y)]

    def source_of(k, j):
        return src_s[1, y_starts[j] + zc_at(k)]

    def gather_z(x, staged, k):
        for i in range(half):
            tile = block_tile(staged, source_of(k, 2 * i))
            if isinstance(k, int):
                kb[x, 0, i] = tile
            else:
                ka[x, k, i] = tile

    def gather_y(x, staged, i):
        def step(k, carry):
            va[x, i, k] = block_tile(staged, source_of(k, 2 * i + 1))
            return carry

        lax.fori_loop(0, n_zc, step, 0, unroll=4)

    def z_sends(x, staged, first, last):
        def step(n, carry):
            away = (n + 1) // 2
            k = n_zc // 2 + jnp.where(lax.rem(n, 2) == 1, away, -away)
            gather_z(x, staged, k)
            z_first(x, k).start()
            return carry

        lax.fori_loop(first, last, step, 0)

    def z_first(x, k):
        return pltpu.make_async_remote_copy(
            src_ref=ka.at[x, k],
            dst_ref=kb.at[x, k],
            send_sem=z_send.at[x, 0, k],
            recv_sem=z_recv.at[x, 0, k],
            device_id=zc_dev(k),
            device_id_type=MESH,
        )

    def y_first(x, i):
        return remote(
            va.at[x, i], vb.at[x, i], y_send.at[x, 0, i], y_recv.at[x, 0, i], y_dev(2 * i + 1)
        )

    def y_second(x, out, i):
        return remote(
            kb.at[x, :, i], out.at[0, i], y_send.at[x, 1, i], y_recv.at[x, 1, i], y_dev(2 * i)
        )

    def z_second(x, out, k):
        return remote(
            vb.at[x, :, k], out.at[1, :, k], z_send.at[x, 1, k], z_recv.at[x, 1, k], zc_dev(k)
        )

    local_copies = []

    def keep(src, dst):
        copy = pltpu.make_async_copy(src, dst, local_sem.at[3 + len(local_copies)])
        copy.start()
        local_copies.append(copy)

    k32[pl.ds(1, n_tp * own_blocks)] = kp[...].astype(F32).reshape(n_tp * own_blocks, TOK, PIECE)
    to_scalar.wait()

    ky1, vy1 = [], []
    kz1 = [z_first(0, k) for k in range(1, n_zc)]
    vz1 = [z_first(1, k) for k in range(1, n_zc)]
    per = -(-(n_zc - 1) // half)
    for n, i in enumerate(odd_order):
        gather_y(0, k32, i)
        ky1.append(y_first(0, i))
        z_sends(0, k32, n * per, min(n_zc - 1, (n + 1) * per))
    gather_z(0, k32, 0)

    own_v.wait()
    for copy in v_copies:
        copy.wait_recv()
    v32[pl.ds(1, n_tp * own_blocks)] = vp[...].astype(F32).reshape(n_tp * own_blocks, TOK, PIECE)
    z_sends(1, v32, 0, n_zc - 1)
    gather_z(1, v32, 0)
    for i in range(half):
        gather_y(1, v32, i)

    for copy in mx_copies:
        copy.wait_recv()
    row_max = mx[0]
    for k in range(1, n_zc):
        row_max = jnp.maximum(row_max, mx[k])
    my_buf[0] = row_max
    my_copies = [
        remote(my_buf.at[0], my_buf.at[j], my_send.at[j], my_recv.at[j], y_dev(j)) for j in y_order
    ]
    for copy in sl_copies:
        copy.wait_recv()
    for k in range(n_zc):
        sy[0, pl.ds(k, 1), :] = sl[k]
    sy_copies = [
        remote(sy.at[0], sy.at[j], sy_send.at[j], sy_recv.at[j], y_dev(j)) for j in y_order
    ]
    for i in odd_order:
        vy1.append(y_first(1, i))
    for copy in my_copies:
        copy.wait_recv()
    all_max = my_buf[0]
    for j in range(1, n_y):
        all_max = jnp.maximum(all_max, my_buf[j])

    chunk = D // n_zc
    row_tops = []
    for h in range(LOCAL_HEADS):
        row_top = jnp.maximum(
            all_max[h : h + 1, :], jnp.max(fresh_scores[h], axis=0, keepdims=True)
        )
        row_tops.append(row_top)
        weights = jnp.exp(scores[h] - row_top)
        su[mzc, pl.ds(h, 1), :] = jnp.sum(weights, axis=0, keepdims=True)
        number = lax.dot_general(
            vp[:, pl.ds(h * D, D)], weights.astype(BF16), TN, preferred_element_type=F32
        )
        for p in range(n_zc):
            rs_src[p, pl.ds(h * chunk, chunk), :] = number[p * chunk : (p + 1) * chunk, :]
    rs_copies = [
        remote(rs_src.at[zc_at(k)], rs_buf.at[mzc], rs_send.at[k], rs_recv.at[k], zc_dev(k))
        for k in z_order
    ]
    su_copies = [
        remote(su.at[mzc], su.at[mzc], su_send.at[k], su_recv.at[k], zc_dev(k)) for k in z_order
    ]
    rs_buf[mzc] = rs_src[mzc]

    for copy in kz1:
        copy.wait_recv()
    ky2 = [y_second(0, kc, i) for i in even_order]
    keep(kb.at[0, :, 0], kc.at[0, 0])
    for copy in ky1:
        copy.wait_recv()
    kz2 = [z_second(0, kc, k) for k in z_order]
    keep(vb.at[0, :, 0], kc.at[1, :, 0])

    fresh_totals = []
    for h in range(LOCAL_HEADS):
        weights = jnp.exp(fresh_scores[h] - row_tops[h])
        fresh_totals.append(jnp.sum(weights, axis=0, keepdims=True))
        number = lax.dot_general(
            fresh_vs[:, pl.ds(h * D, D)], weights.astype(BF16), TN, preferred_element_type=F32
        )
        for p in range(n_zc):
            fresh_num[p, pl.ds(h * chunk, chunk), :] = number[p * chunk : (p + 1) * chunk, :]

    for copy in sy_copies:
        copy.wait_recv()
    column = []
    for j in range(n_y):
        first_place = (j % 2) * half * n_zc + (j // 2) * n_zc + 1
        lists = sy[j]
        wide = lax.broadcasted_iota(jnp.int32, (n_zc, D), 1)
        picked = jnp.sum(jnp.where(wide == me, lists, 0), axis=1, keepdims=True)
        index = lax.broadcasted_iota(jnp.int32, (n_zc, D), 0) + first_place
        found = jnp.where(picked == wide + 1, index, 0)
        column.append(jnp.max(found, axis=0, keepdims=True))
    arrival = column[0]
    for j in range(1, n_y):
        arrival = jnp.maximum(arrival, column[j])
    arrival_ref[...] = jnp.broadcast_to(arrival, (8, D))

    for copy in rs_copies:
        copy.wait_recv()
    part = rs_buf[0]
    for p in range(1, n_zc):
        part = part + rs_buf[p]
    yy_buf[my] = part
    yy_copies = [
        remote(yy_buf.at[my], yy_buf.at[my], yy_send.at[j], yy_recv.at[j], y_dev(j)) for j in y_order
    ]
    for copy in su_copies:
        copy.wait_recv()
    part = su[0]
    for p in range(1, n_zc):
        part = part + su[p]
    sv[my] = part
    sv_copies = [
        remote(sv.at[my], sv.at[my], sv_send.at[j], sv_recv.at[j], y_dev(j)) for j in y_order
    ]

    for copy in vz1:
        copy.wait_recv()
    vy2 = [y_second(1, vc, i) for i in even_order]
    keep(kb.at[1, :, 0], vc.at[0, 0])
    for copy in vy1:
        copy.wait_recv()
    vz2 = [z_second(1, vc, k) for k in z_order[: n_zc // 2]]
    keep(vb.at[1, :, 0], vc.at[1, :, 0])

    for copy in yy_copies:
        copy.wait_recv()
    whole = yy_buf[0]
    for copy in sv_copies:
        copy.wait_recv()
    sums = sv[0]
    for j in range(1, n_y):
        whole = whole + yy_buf[j]
        sums = sums + sv[j]
    norms = []
    for h in range(LOCAL_HEADS):
        total = sums[h : h + 1, :] + fresh_totals[h]
        number = whole[h * chunk : (h + 1) * chunk, :] + fresh_num[mzc, pl.ds(h * chunk, chunk), :]
        ag_buf[mzc, pl.ds(h * chunk, chunk), :] = number / total
        norms.append(row_tops[h] + jnp.log(total))
    ag_copies = [
        remote(ag_buf.at[mzc], ag_buf.at[mzc], ag_send.at[k], ag_recv.at[k], zc_dev(k))
        for k in z_order
    ]
    vz2 += [z_second(1, vc, k) for k in z_order[n_zc // 2 :]]
    wide_lane = lax.broadcasted_iota(jnp.int32, (SR, D), 1)
    wide_row = lax.broadcasted_iota(jnp.int32, (SR, D), 0)
    by_head = jnp.zeros((SR, D), F32)
    for h in range(LOCAL_HEADS):
        for g in range(GROUP):
            picked = jnp.where(wide_lane == wide_row + g * SR, norms[h], 0.0)
            value = jnp.sum(picked, axis=1, keepdims=True)
            by_head = jnp.where(wide_lane == h * GROUP + g, value, by_head)
    norm_ref[...] = by_head
    for copy in (
        meta_copies
        + k_copies
        + v_copies
        + sl_copies
        + sy_copies
        + mx_copies
        + my_copies
        + kz1
        + ky1
        + vz1
        + vy1
        + rs_copies
        + su_copies
        + yy_copies
        + sv_copies
    ):
        copy.wait_send()
    for copy in kz2 + ky2:
        copy.wait()
    for copy in ag_copies:
        copy.wait_recv()
    for h in range(LOCAL_HEADS):
        by_entry = jnp.concatenate(
            [ag_buf[p, pl.ds(h * chunk, chunk), :] for p in range(n_zc)], axis=0
        )
        by_row = jnp.transpose(by_entry)
        for g in range(GROUP):
            attended_ref[:, pl.ds((h * GROUP + g) * D, D)] = by_row[g * SR : (g + 1) * SR, :]

    for copy in vz2 + vy2:
        copy.wait_recv()
    for copy in local_copies:
        copy.wait()
    for copy in vz2 + vy2 + ag_copies:
        copy.wait_send()


def place_kernel(
    slot_count,
    arrival_ref,
    rows_ref,
    norm_ref,
    k_ref,
    v_ref,
    attended_ref,
    log_norm_ref,
    out_k_ref,
    out_v_ref,
):
    for s in range(STEPS):
        attended_ref[s] = rows_ref[pl.ds(s * REQUESTS, REQUESTS), :]
        log_norm_ref[s] = norm_ref[pl.ds(s * REQUESTS, REQUESTS), pl.ds(0, LOCAL_HEADS * GROUP)]

    def place(s, carry):
        index = arrival_ref[0, s]
        at = jnp.maximum(index - 1, 0)
        there = index > 0
        for ref, out in ((k_ref, out_k_ref), (v_ref, out_v_ref)):
            tile = ref[at].astype(F32)
            wide = jnp.concatenate([tile[:TOK, :], tile[TOK:, :]], axis=1)
            out[s] = jnp.where(there, wide, 0.0).astype(BF16)
        return carry

    lax.fori_loop(0, slot_count, place, 0, unroll=4)


def on_device(
    n_y,
    n_zc,
    prefilled_block_keys,
    prefilled_block_values,
    queries,
    step_token_keys,
    step_token_values,
    lengths,
    block_request,
    block_number,
    owner_rank,
    owner_slot,
    group_first,
):
    n_tp = lax.axis_size("tp")
    own_blocks, _, full_width = prefilled_block_keys.shape
    row_blocks = own_blocks * n_tp
    tokens = own_blocks * TOK
    slot_count = 2 * row_blocks
    n_sp = n_y * n_zc
    chunk = D // n_zc
    smem = pl.BlockSpec(memory_space=pltpu.SMEM)
    vmem = pl.BlockSpec(memory_space=pltpu.VMEM)
    hbm = pl.BlockSpec(memory_space=pltpu.HBM)
    half = n_y // 2
    dma = pltpu.SemaphoreType.DMA
    attended, norms, arrival, kc, vc = pl.pallas_call(
        functools.partial(exchange_kernel, n_y, n_zc, n_tp, own_blocks),
        out_shape=(
            jax.ShapeDtypeStruct((SR, GROUP * PIECE), F32),
            jax.ShapeDtypeStruct((SR, D), F32),
            jax.ShapeDtypeStruct((8, D), jnp.int32),
            jax.ShapeDtypeStruct((2, half, n_zc, 2 * TOK, D), BF16),
            jax.ShapeDtypeStruct((2, half, n_zc, 2 * TOK, D), BF16),
        ),
        in_specs=[hbm] * 11,
        out_specs=(vmem,) * 5,
        scratch_shapes=[
            pltpu.VMEM((n_tp, 8, D), jnp.int32),
            pltpu.VMEM((n_tp * tokens, PIECE), BF16),
            pltpu.VMEM((n_tp * tokens, PIECE), BF16),
            pltpu.VMEM((row_blocks + 1, TOK, PIECE), F32),
            pltpu.VMEM((row_blocks + 1, TOK, PIECE), F32),
            pltpu.VMEM((8, D), jnp.int32),
            pltpu.SMEM((8, D), jnp.int32),
            pltpu.VMEM((LOCAL_HEADS, n_tp * tokens, ROWS), F32),
            pltpu.VMEM((2, n_zc, half, 2 * TOK, D), BF16),
            pltpu.VMEM((2, n_zc, half, 2 * TOK, D), BF16),
            pltpu.VMEM((2, half, n_zc, 2 * TOK, D), BF16),
            pltpu.VMEM((2, half, n_zc, 2 * TOK, D), BF16),
            pltpu.SMEM((own_blocks,), jnp.int32),
            pltpu.SMEM((own_blocks,), jnp.int32),
            pltpu.SMEM((own_blocks,), jnp.int32),
            pltpu.SMEM((own_blocks,), jnp.int32),
            pltpu.SMEM((REQUESTS,), jnp.int32),
            pltpu.SMEM((REQUESTS,), jnp.int32),
            pltpu.VMEM((STEPS, REQUESTS, GROUP * PIECE), BF16),
            pltpu.VMEM((STEPS, REQUESTS, PIECE), BF16),
            pltpu.VMEM((STEPS, REQUESTS, PIECE), BF16),
            dma((9,)),
            pltpu.VMEM((SR, GROUP * PIECE), BF16),
            pltpu.VMEM((SR, PIECE), BF16),
            pltpu.VMEM((SR, PIECE), BF16),
            pltpu.VMEM((n_zc, 1, D), jnp.int32),
            pltpu.VMEM((n_y, n_zc, D), jnp.int32),
            pltpu.VMEM((n_zc, LOCAL_HEADS, ROWS), F32),
            pltpu.VMEM((n_y, LOCAL_HEADS, ROWS), F32),
            pltpu.VMEM((n_zc, LOCAL_HEADS, ROWS), F32),
            pltpu.VMEM((n_y, LOCAL_HEADS, ROWS), F32),
            pltpu.VMEM((n_zc, LOCAL_HEADS * chunk, ROWS), F32),
            pltpu.VMEM((n_zc, LOCAL_HEADS * chunk, ROWS), F32),
            pltpu.VMEM((n_zc, LOCAL_HEADS * chunk, ROWS), F32),
            pltpu.VMEM((n_y, LOCAL_HEADS * chunk, ROWS), F32),
            pltpu.VMEM((n_zc, LOCAL_HEADS * chunk, ROWS), F32),
            dma((7,)),
        ]
        + [dma((n_tp,))] * 6
        + [dma((n_zc,))] * 2
        + [dma((n_y,))] * 2
        + [dma((n_zc,))] * 2
        + [dma((n_y,))] * 2
        + [dma((n_zc,))] * 2
        + [dma((n_y,))] * 2
        + [dma((2, 2, n_zc))] * 2
        + [dma((2, 2, half))] * 2
        + [dma((n_zc,))] * 2
        + [dma((n_y,))] * 2
        + [dma((n_zc,))] * 2,
        compiler_params=pltpu.CompilerParams(
            collective_id=0, has_side_effects=True, vmem_limit_bytes=40 * 2**20
        ),
        name="exchange",
    )(
        *[
            pltpu.with_memory_space_constraint(operand, pltpu.HBM)
            for operand in (
                block_request,
                block_number,
                owner_rank,
                owner_slot,
                lengths,
                group_first,
                queries,
                step_token_keys,
                step_token_values,
                prefilled_block_keys.reshape(tokens, full_width),
                prefilled_block_values.reshape(tokens, full_width),
            )
        ]
    )
    slot_shape = jax.ShapeDtypeStruct((slot_count, TOK, PIECE), BF16)
    return pl.pallas_call(
        functools.partial(place_kernel, slot_count),
        out_shape=(
            jax.ShapeDtypeStruct((STEPS, REQUESTS, GROUP * PIECE), F32),
            jax.ShapeDtypeStruct((STEPS, REQUESTS, LOCAL_HEADS * GROUP), F32),
            slot_shape,
            slot_shape,
        ),
        in_specs=[smem] + [vmem] * 4,
        out_specs=(vmem,) * 4,
        compiler_params=pltpu.CompilerParams(vmem_limit_bytes=16 * 2**20),
        name="place",
    )(
        arrival,
        attended,
        norms,
        kc.reshape(n_sp, 2 * TOK, D),
        vc.reshape(n_sp, 2 * TOK, D),
    )


def solution(mesh):
    sp = mesh.shape["sp"]
    n_y = max(2, sp // 16)
    return jax.shard_map(
        functools.partial(on_device, n_y, sp // n_y),
        mesh=mesh,
        in_specs=(
            P(("sp", "tp"), None, None),
            P(("sp", "tp"), None, None),
            P(None, None, "tp"),
            P(None, None, "tp"),
            P(None, None, "tp"),
            P(),
            P(("sp", "tp")),
            P(("sp", "tp")),
            P(("sp", "tp")),
            P(("sp", "tp")),
            P(),
        ),
        out_specs=(
            P(None, None, "tp"),
            P(None, None, "tp"),
            P("sp", None, "tp"),
            P("sp", None, "tp"),
        ),
        check_vma=False,
    )
```

```python
import functools
import math

import jax
import jax.numpy as jnp
from jax import lax
from jax.experimental import pallas as pl
from jax.experimental.pallas import tpu as pltpu
from jax.sharding import PartitionSpec as P

D = 128
TOK = 8
STEPS = 4
REQUESTS = 4
SR = STEPS * REQUESTS
GROUP = 8
ROWS = GROUP * SR
LOCAL_HEADS = 2
PIECE = LOCAL_HEADS * D
NEGATIVE = -1e30
SCALE = 1.0 / math.sqrt(D)
MESH = pl.DeviceIdType.MESH
F32 = jnp.float32
BF16 = jnp.bfloat16
NT = (((1,), (1,)), ((), ()))
TN = (((0,), (0,)), ((), ()))


def exchange_kernel(
    n_y,
    n_zc,
    n_tp,
    own_blocks,
    request_hbm,
    number_hbm,
    rank_hbm,
    slot_hbm,
    lengths_hbm,
    first_hbm,
    q_hbm,
    fresh_k_hbm,
    fresh_v_hbm,
    keys_ref,
    values_ref,
    attended_ref,
    norm_ref,
    arrival_ref,
    kc,
    vc,
    meta,
    kp,
    vp,
    k32,
    v32,
    src_v,
    src_s,
    scores,
    ka,
    kb,
    va,
    vb,
    request_ref,
    number_ref,
    rank_ref,
    slot_ref,
    lengths_ref,
    first_ref,
    q_ref,
    fresh_k_ref,
    fresh_v_ref,
    operand_sem,
    qs,
    fresh_ks,
    fresh_vs,
    sl,
    sy,
    su,
    sv,
    mx,
    my_buf,
    fresh_num,
    rs_src,
    rs_buf,
    yy_buf,
    ag_buf,
    local_sem,
    meta_send,
    meta_recv,
    kp_send,
    kp_recv,
    vp_send,
    vp_recv,
    sl_send,
    sl_recv,
    sy_send,
    sy_recv,
    su_send,
    su_recv,
    sv_send,
    sv_recv,
    mx_send,
    mx_recv,
    my_send,
    my_recv,
    z_send,
    z_recv,
    y_send,
    y_recv,
    rs_send,
    rs_recv,
    yy_send,
    yy_recv,
    ag_send,
    ag_recv,
):
    me = lax.axis_index("sp")
    tp = lax.axis_index("tp")
    my = me // n_zc
    mzc = lax.rem(me, n_zc)
    tokens = own_blocks * TOK

    def zc_at(k):
        return lax.rem(mzc + k, n_zc)

    def y_at(j):
        return lax.rem(my + j, n_y)

    def tp_at(k):
        return lax.rem(tp + k, n_tp)

    z_order = sorted(range(1, n_zc), key=lambda k: -min(k, n_zc - k))
    y_order = sorted(range(1, n_y), key=lambda j: -min(j, n_y - j))
    odd_order = [(j - 1) // 2 for j in y_order if j % 2]
    even_order = [j // 2 for j in y_order if j % 2 == 0]

    def zc_dev(k):
        return (my * n_zc + zc_at(k), tp)

    def y_dev(j):
        return (y_at(j) * n_zc + mzc, tp)

    def tp_dev(k):
        return (me, tp_at(k))

    def remote(src, dst, send, recv, dev):
        copy = pltpu.make_async_remote_copy(
            src_ref=src, dst_ref=dst, send_sem=send, recv_sem=recv, device_id=dev, device_id_type=MESH
        )
        copy.start()
        return copy

    barrier = pltpu.get_barrier_semaphore()
    distant = [(min(k, n_zc - k) // 2, zc_dev(k)) for k in z_order]
    distant += [(min(j, n_y - j), y_dev(j)) for j in y_order]
    distant += [(min(k, n_tp - k), tp_dev(k)) for k in range(1, n_tp)]
    peers = [dev for _, dev in sorted(distant, key=lambda pair: -pair[0])]
    for dev in peers:
        pl.semaphore_signal(barrier, inc=1, device_id=dev, device_id_type=MESH)

    def columns(t):
        return pl.ds(pl.multiple_of(t * PIECE, PIECE), PIECE)

    def rows_of(t):
        return pl.ds(pl.multiple_of(t * tokens, tokens), tokens)

    own_k = pltpu.make_async_copy(keys_ref.at[:, columns(tp)], kp.at[rows_of(tp)], local_sem.at[0])
    own_v = pltpu.make_async_copy(values_ref.at[:, columns(tp)], vp.at[rows_of(tp)], local_sem.at[1])
    own_k.start()
    own_v.start()

    fetches = [
        pltpu.make_async_copy(src, dst, operand_sem.at[n])
        for n, (src, dst) in enumerate(
            (
                (request_hbm, request_ref),
                (number_hbm, number_ref),
                (rank_hbm, rank_ref),
                (slot_hbm, slot_ref),
                (lengths_hbm, lengths_ref),
                (first_hbm, first_ref),
                (q_hbm, q_ref),
                (fresh_k_hbm, fresh_k_ref),
                (fresh_v_hbm, fresh_v_ref),
            )
        )
    ]
    for fetch in fetches:
        fetch.start()
    for fetch in fetches:
        fetch.wait()

    lane = lax.broadcasted_iota(jnp.int32, (1, D), 1)
    codes = jnp.full((1, D), REQUESTS, jnp.int32)
    sources = jnp.zeros((1, D), jnp.int32)
    slots = jnp.zeros((1, D), jnp.int32)
    for b in range(own_blocks):
        request = request_ref[b]
        owner = first_ref[request] + rank_ref[b]
        place = number_ref[b] * TOK + (lane - b * TOK)
        mine = (lane >= b * TOK) & (lane < (b + 1) * TOK) & (place < lengths_ref[request])
        codes = jnp.where(mine, request, codes)
        hit = lane == owner
        sources = jnp.where(hit, tp * own_blocks + b + 1, sources)
        slots = jnp.where(hit, slot_ref[b] + 1, slots)
    own_meta = jnp.concatenate(
        [codes, sources, slots, jnp.zeros((5, D), jnp.int32)], axis=0
    )
    meta[tp] = own_meta

    row_lane = lax.broadcasted_iota(jnp.int32, (1, ROWS), 1)
    row_request = lax.rem(row_lane, REQUESTS)
    row_step = lax.rem(row_lane, SR) // REQUESTS
    row_code = row_request.astype(F32)

    def stack_steps(ref, out):
        out[...] = jnp.concatenate([ref[s].astype(F32) for s in range(STEPS)], axis=0).astype(BF16)

    stack_steps(q_ref, qs)
    stack_steps(fresh_k_ref, fresh_ks)
    stack_steps(fresh_v_ref, fresh_vs)

    def q_head(h):
        return jnp.concatenate(
            [qs[:, pl.ds((h * GROUP + g) * D, D)] for g in range(GROUP)], axis=0
        )

    fresh_row = lax.broadcasted_iota(jnp.int32, (SR, ROWS), 0)
    fresh_ok = (lax.rem(fresh_row, REQUESTS) == row_request) & (fresh_row // REQUESTS <= row_step)
    fresh_scores = []
    for h in range(LOCAL_HEADS):
        dots = lax.dot_general(
            fresh_ks[:, pl.ds(h * D, D)], q_head(h), NT, preferred_element_type=F32
        )
        fresh_scores.append(jnp.where(fresh_ok, dots * SCALE, NEGATIVE))

    k32[0] = jnp.zeros((TOK, PIECE), F32)
    v32[0] = jnp.zeros((TOK, PIECE), F32)

    pl.semaphore_wait(barrier, len(peers))

    meta_copies, k_copies, v_copies = [], [], []
    for k in range(1, n_tp):
        meta_copies.append(
            remote(meta.at[tp], meta.at[tp], meta_send.at[k], meta_recv.at[k], tp_dev(k))
        )
    for k in range(1, n_tp):
        k_copies.append(
            remote(keys_ref.at[:, columns(tp_at(k))], kp.at[rows_of(tp)], kp_send.at[k], kp_recv.at[k], tp_dev(k))
        )
    for k in range(1, n_tp):
        v_copies.append(
            remote(
                values_ref.at[:, columns(tp_at(k))], vp.at[rows_of(tp)], vp_send.at[k], vp_recv.at[k], tp_dev(k)
            )
        )

    for copy in meta_copies:
        copy.wait_recv()
    row_meta = meta[0]
    for t in range(1, n_tp):
        row_meta = jnp.maximum(row_meta, meta[t])
    src_v[...] = row_meta
    to_scalar = pltpu.make_async_copy(src_v, src_s, local_sem.at[2])
    to_scalar.start()
    sl[0] = row_meta[2:3, :]
    sl_copies = [
        remote(sl.at[0], sl.at[k], sl_send.at[k], sl_recv.at[k], zc_dev(k)) for k in z_order
    ]
    code_column = jnp.concatenate(
        [
            jnp.transpose(jnp.broadcast_to(meta[t][0:1, :].astype(F32), (D, D)))[:tokens, :]
            for t in range(n_tp)
        ],
        axis=0,
    )
    allowed = code_column == row_code

    own_k.wait()
    for copy in k_copies:
        copy.wait_recv()
    for h in range(LOCAL_HEADS):
        dots = lax.dot_general(kp[:, pl.ds(h * D, D)], q_head(h), NT, preferred_element_type=F32)
        masked = jnp.where(allowed, dots * SCALE, NEGATIVE)
        scores[h] = masked
        mx[0, pl.ds(h, 1), :] = jnp.max(masked, axis=0, keepdims=True)
    mx_copies = [
        remote(mx.at[0], mx.at[k], mx_send.at[k], mx_recv.at[k], zc_dev(k)) for k in z_order
    ]

    def block_tile(ref, index):
        block = ref[index]
        return jnp.concatenate([block[:, :D], block[:, D:]], axis=0).astype(BF16)

    half = n_y // 2
    y_starts = [y_at(j) * n_zc for j in range(n_y)]

    def source_of(k, j):
        return src_s[1, y_starts[j] + zc_at(k)]

    def gather_z(x, staged, k):
        for i in range(half):
            tile = block_tile(staged, source_of(k, 2 * i))
            if isinstance(k, int):
                kb[x, 0, i] = tile
            else:
                ka[x, k, i] = tile

    def gather_y(x, staged, i):
        def step(k, carry):
            va[x, i, k] = block_tile(staged, source_of(k, 2 * i + 1))
            return carry

        lax.fori_loop(0, n_zc, step, 0, unroll=4)

    def z_sends(x, staged, first, last):
        def step(n, carry):
            away = (n + 1) // 2
            k = n_zc // 2 + jnp.where(lax.rem(n, 2) == 1, away, -away)
            gather_z(x, staged, k)
            z_first(x, k).start()
            return carry

        lax.fori_loop(first, last, step, 0)

    def z_first(x, k):
        return pltpu.make_async_remote_copy(
            src_ref=ka.at[x, k],
            dst_ref=kb.at[x, k],
            send_sem=z_send.at[x, 0, k],
            recv_sem=z_recv.at[x, 0, k],
            device_id=zc_dev(k),
            device_id_type=MESH,
        )

    def y_first(x, i):
        return remote(
            va.at[x, i], vb.at[x, i], y_send.at[x, 0, i], y_recv.at[x, 0, i], y_dev(2 * i + 1)
        )

    def y_second(x, out, i):
        return remote(
            kb.at[x, :, i], out.at[0, i], y_send.at[x, 1, i], y_recv.at[x, 1, i], y_dev(2 * i)
        )

    def z_second(x, out, k):
        return remote(
            vb.at[x, :, k], out.at[1, :, k], z_send.at[x, 1, k], z_recv.at[x, 1, k], zc_dev(k)
        )

    local_copies = []

    def keep(src, dst):
        copy = pltpu.make_async_copy(src, dst, local_sem.at[3 + len(local_copies)])
        copy.start()
        local_copies.append(copy)

    k32[pl.ds(1, n_tp * own_blocks)] = kp[...].astype(F32).reshape(n_tp * own_blocks, TOK, PIECE)
    to_scalar.wait()

    ky1, vy1 = [], []
    kz1 = [z_first(0, k) for k in range(1, n_zc)]
    vz1 = [z_first(1, k) for k in range(1, n_zc)]
    per = -(-(n_zc - 1) // half)
    for n, i in enumerate(odd_order):
        gather_y(0, k32, i)
        ky1.append(y_first(0, i))
        z_sends(0, k32, n * per, min(n_zc - 1, (n + 1) * per))
    gather_z(0, k32, 0)

    own_v.wait()
    for copy in v_copies:
        copy.wait_recv()
    v32[pl.ds(1, n_tp * own_blocks)] = vp[...].astype(F32).reshape(n_tp * own_blocks, TOK, PIECE)
    z_sends(1, v32, 0, n_zc - 1)
    gather_z(1, v32, 0)
    for i in range(half):
        gather_y(1, v32, i)

    for copy in mx_copies:
        copy.wait_recv()
    row_max = mx[0]
    for k in range(1, n_zc):
        row_max = jnp.maximum(row_max, mx[k])
    my_buf[0] = row_max
    my_copies = [
        remote(my_buf.at[0], my_buf.at[j], my_send.at[j], my_recv.at[j], y_dev(j)) for j in y_order
    ]
    for i in odd_order:
        vy1.append(y_first(1, i))
    for copy in my_copies:
        copy.wait_recv()
    all_max = my_buf[0]
    for j in range(1, n_y):
        all_max = jnp.maximum(all_max, my_buf[j])

    chunk = D // n_zc
    row_tops = []
    for h in range(LOCAL_HEADS):
        row_top = jnp.maximum(
            all_max[h : h + 1, :], jnp.max(fresh_scores[h], axis=0, keepdims=True)
        )
        row_tops.append(row_top)
        weights = jnp.exp(scores[h] - row_top)
        su[mzc, pl.ds(h, 1), :] = jnp.sum(weights, axis=0, keepdims=True)
        number = lax.dot_general(
            vp[:, pl.ds(h * D, D)], weights.astype(BF16), TN, preferred_element_type=F32
        )
        for p in range(n_zc):
            rs_src[p, pl.ds(h * chunk, chunk), :] = number[p * chunk : (p + 1) * chunk, :]
    rs_copies = [
        remote(rs_src.at[zc_at(k)], rs_buf.at[mzc], rs_send.at[k], rs_recv.at[k], zc_dev(k))
        for k in z_order
    ]
    su_copies = [
        remote(su.at[mzc], su.at[mzc], su_send.at[k], su_recv.at[k], zc_dev(k)) for k in z_order
    ]
    rs_buf[mzc] = rs_src[mzc]

    for copy in kz1:
        copy.wait_recv()
    ky2 = [y_second(0, kc, i) for i in even_order]
    keep(kb.at[0, :, 0], kc.at[0, 0])
    for copy in sl_copies:
        copy.wait_recv()
    for k in range(n_zc):
        sy[0, pl.ds(k, 1), :] = sl[k]
    sy_copies = [
        remote(sy.at[0], sy.at[j], sy_send.at[j], sy_recv.at[j], y_dev(j)) for j in y_order
    ]
    for copy in ky1:
        copy.wait_recv()
    kz2 = [z_second(0, kc, k) for k in z_order]
    keep(vb.at[0, :, 0], kc.at[1, :, 0])

    fresh_totals = []
    for h in range(LOCAL_HEADS):
        weights = jnp.exp(fresh_scores[h] - row_tops[h])
        fresh_totals.append(jnp.sum(weights, axis=0, keepdims=True))
        number = lax.dot_general(
            fresh_vs[:, pl.ds(h * D, D)], weights.astype(BF16), TN, preferred_element_type=F32
        )
        for p in range(n_zc):
            fresh_num[p, pl.ds(h * chunk, chunk), :] = number[p * chunk : (p + 1) * chunk, :]


    for copy in rs_copies:
        copy.wait_recv()
    part = rs_buf[0]
    for p in range(1, n_zc):
        part = part + rs_buf[p]
    yy_buf[my] = part
    yy_copies = [
        remote(yy_buf.at[my], yy_buf.at[my], yy_send.at[j], yy_recv.at[j], y_dev(j)) for j in y_order
    ]
    for copy in su_copies:
        copy.wait_recv()
    part = su[0]
    for p in range(1, n_zc):
        part = part + su[p]
    sv[my] = part
    sv_copies = [
        remote(sv.at[my], sv.at[my], sv_send.at[j], sv_recv.at[j], y_dev(j)) for j in y_order
    ]

    for copy in vz1:
        copy.wait_recv()
    vy2 = [y_second(1, vc, i) for i in even_order]
    keep(kb.at[1, :, 0], vc.at[0, 0])
    for copy in vy1:
        copy.wait_recv()
    vz2 = [z_second(1, vc, k) for k in z_order[: n_zc // 2]]
    keep(vb.at[1, :, 0], vc.at[1, :, 0])

    for copy in yy_copies:
        copy.wait_recv()
    whole = yy_buf[0]
    for copy in sv_copies:
        copy.wait_recv()
    sums = sv[0]
    for j in range(1, n_y):
        whole = whole + yy_buf[j]
        sums = sums + sv[j]
    norms = []
    for h in range(LOCAL_HEADS):
        total = sums[h : h + 1, :] + fresh_totals[h]
        number = whole[h * chunk : (h + 1) * chunk, :] + fresh_num[mzc, pl.ds(h * chunk, chunk), :]
        ag_buf[mzc, pl.ds(h * chunk, chunk), :] = number / total
        norms.append(row_tops[h] + jnp.log(total))
    ag_copies = [
        remote(ag_buf.at[mzc], ag_buf.at[mzc], ag_send.at[k], ag_recv.at[k], zc_dev(k))
        for k in z_order
    ]
    vz2 += [z_second(1, vc, k) for k in z_order[n_zc // 2 :]]
    for copy in sy_copies:
        copy.wait_recv()
    column = []
    for j in range(n_y):
        first_place = (j % 2) * half * n_zc + (j // 2) * n_zc + 1
        lists = sy[j]
        wide = lax.broadcasted_iota(jnp.int32, (n_zc, D), 1)
        picked = jnp.sum(jnp.where(wide == me, lists, 0), axis=1, keepdims=True)
        index = lax.broadcasted_iota(jnp.int32, (n_zc, D), 0) + first_place
        found = jnp.where(picked == wide + 1, index, 0)
        column.append(jnp.max(found, axis=0, keepdims=True))
    arrival = column[0]
    for j in range(1, n_y):
        arrival = jnp.maximum(arrival, column[j])
    arrival_ref[...] = jnp.broadcast_to(arrival, (8, D))
    wide_lane = lax.broadcasted_iota(jnp.int32, (SR, D), 1)
    wide_row = lax.broadcasted_iota(jnp.int32, (SR, D), 0)
    by_head = jnp.zeros((SR, D), F32)
    for h in range(LOCAL_HEADS):
        for g in range(GROUP):
            picked = jnp.where(wide_lane == wide_row + g * SR, norms[h], 0.0)
            value = jnp.sum(picked, axis=1, keepdims=True)
            by_head = jnp.where(wide_lane == h * GROUP + g, value, by_head)
    norm_ref[...] = by_head
    for copy in (
        meta_copies
        + k_copies
        + v_copies
        + sl_copies
        + sy_copies
        + mx_copies
        + my_copies
        + kz1
        + ky1
        + vz1
        + vy1
        + rs_copies
        + su_copies
        + yy_copies
        + sv_copies
    ):
        copy.wait_send()
    for copy in kz2 + ky2:
        copy.wait()
    for copy in ag_copies:
        copy.wait_recv()
    for h in range(LOCAL_HEADS):
        by_entry = jnp.concatenate(
            [ag_buf[p, pl.ds(h * chunk, chunk), :] for p in range(n_zc)], axis=0
        )
        by_row = jnp.transpose(by_entry)
        for g in range(GROUP):
            attended_ref[:, pl.ds((h * GROUP + g) * D, D)] = by_row[g * SR : (g + 1) * SR, :]

    for copy in vz2 + vy2:
        copy.wait_recv()
    for copy in local_copies:
        copy.wait()
    for copy in vz2 + vy2 + ag_copies:
        copy.wait_send()


def place_kernel(
    slot_count,
    arrival_ref,
    rows_ref,
    norm_ref,
    k_ref,
    v_ref,
    attended_ref,
    log_norm_ref,
    out_k_ref,
    out_v_ref,
):
    for s in range(STEPS):
        attended_ref[s] = rows_ref[pl.ds(s * REQUESTS, REQUESTS), :]
        log_norm_ref[s] = norm_ref[pl.ds(s * REQUESTS, REQUESTS), pl.ds(0, LOCAL_HEADS * GROUP)]

    def place(s, carry):
        index = arrival_ref[0, s]
        at = jnp.maximum(index - 1, 0)
        there = index > 0
        for ref, out in ((k_ref, out_k_ref), (v_ref, out_v_ref)):
            tile = ref[at].astype(F32)
            wide = jnp.concatenate([tile[:TOK, :], tile[TOK:, :]], axis=1)
            out[s] = jnp.where(there, wide, 0.0).astype(BF16)
        return carry

    lax.fori_loop(0, slot_count, place, 0, unroll=16)


def on_device(
    n_y,
    n_zc,
    prefilled_block_keys,
    prefilled_block_values,
    queries,
    step_token_keys,
    step_token_values,
    lengths,
    block_request,
    block_number,
    owner_rank,
    owner_slot,
    group_first,
):
    n_tp = lax.axis_size("tp")
    own_blocks, _, full_width = prefilled_block_keys.shape
    row_blocks = own_blocks * n_tp
    tokens = own_blocks * TOK
    slot_count = 2 * row_blocks
    n_sp = n_y * n_zc
    chunk = D // n_zc
    smem = pl.BlockSpec(memory_space=pltpu.SMEM)
    vmem = pl.BlockSpec(memory_space=pltpu.VMEM)
    hbm = pl.BlockSpec(memory_space=pltpu.HBM)
    half = n_y // 2
    dma = pltpu.SemaphoreType.DMA
    attended, norms, arrival, kc, vc = pl.pallas_call(
        functools.partial(exchange_kernel, n_y, n_zc, n_tp, own_blocks),
        out_shape=(
            jax.ShapeDtypeStruct((SR, GROUP * PIECE), F32),
            jax.ShapeDtypeStruct((SR, D), F32),
            jax.ShapeDtypeStruct((8, D), jnp.int32),
            jax.ShapeDtypeStruct((2, half, n_zc, 2 * TOK, D), BF16),
            jax.ShapeDtypeStruct((2, half, n_zc, 2 * TOK, D), BF16),
        ),
        in_specs=[hbm] * 11,
        out_specs=(vmem,) * 5,
        scratch_shapes=[
            pltpu.VMEM((n_tp, 8, D), jnp.int32),
            pltpu.VMEM((n_tp * tokens, PIECE), BF16),
            pltpu.VMEM((n_tp * tokens, PIECE), BF16),
            pltpu.VMEM((row_blocks + 1, TOK, PIECE), F32),
            pltpu.VMEM((row_blocks + 1, TOK, PIECE), F32),
            pltpu.VMEM((8, D), jnp.int32),
            pltpu.SMEM((8, D), jnp.int32),
            pltpu.VMEM((LOCAL_HEADS, n_tp * tokens, ROWS), F32),
            pltpu.VMEM((2, n_zc, half, 2 * TOK, D), BF16),
            pltpu.VMEM((2, n_zc, half, 2 * TOK, D), BF16),
            pltpu.VMEM((2, half, n_zc, 2 * TOK, D), BF16),
            pltpu.VMEM((2, half, n_zc, 2 * TOK, D), BF16),
            pltpu.SMEM((own_blocks,), jnp.int32),
            pltpu.SMEM((own_blocks,), jnp.int32),
            pltpu.SMEM((own_blocks,), jnp.int32),
            pltpu.SMEM((own_blocks,), jnp.int32),
            pltpu.SMEM((REQUESTS,), jnp.int32),
            pltpu.SMEM((REQUESTS,), jnp.int32),
            pltpu.VMEM((STEPS, REQUESTS, GROUP * PIECE), BF16),
            pltpu.VMEM((STEPS, REQUESTS, PIECE), BF16),
            pltpu.VMEM((STEPS, REQUESTS, PIECE), BF16),
            dma((9,)),
            pltpu.VMEM((SR, GROUP * PIECE), BF16),
            pltpu.VMEM((SR, PIECE), BF16),
            pltpu.VMEM((SR, PIECE), BF16),
            pltpu.VMEM((n_zc, 1, D), jnp.int32),
            pltpu.VMEM((n_y, n_zc, D), jnp.int32),
            pltpu.VMEM((n_zc, LOCAL_HEADS, ROWS), F32),
            pltpu.VMEM((n_y, LOCAL_HEADS, ROWS), F32),
            pltpu.VMEM((n_zc, LOCAL_HEADS, ROWS), F32),
            pltpu.VMEM((n_y, LOCAL_HEADS, ROWS), F32),
            pltpu.VMEM((n_zc, LOCAL_HEADS * chunk, ROWS), F32),
            pltpu.VMEM((n_zc, LOCAL_HEADS * chunk, ROWS), F32),
            pltpu.VMEM((n_zc, LOCAL_HEADS * chunk, ROWS), F32),
            pltpu.VMEM((n_y, LOCAL_HEADS * chunk, ROWS), F32),
            pltpu.VMEM((n_zc, LOCAL_HEADS * chunk, ROWS), F32),
            dma((7,)),
        ]
        + [dma((n_tp,))] * 6
        + [dma((n_zc,))] * 2
        + [dma((n_y,))] * 2
        + [dma((n_zc,))] * 2
        + [dma((n_y,))] * 2
        + [dma((n_zc,))] * 2
        + [dma((n_y,))] * 2
        + [dma((2, 2, n_zc))] * 2
        + [dma((2, 2, half))] * 2
        + [dma((n_zc,))] * 2
        + [dma((n_y,))] * 2
        + [dma((n_zc,))] * 2,
        compiler_params=pltpu.CompilerParams(
            collective_id=0, has_side_effects=True, vmem_limit_bytes=40 * 2**20
        ),
        name="exchange",
    )(
        *[
            pltpu.with_memory_space_constraint(operand, pltpu.HBM)
            for operand in (
                block_request,
                block_number,
                owner_rank,
                owner_slot,
                lengths,
                group_first,
                queries,
                step_token_keys,
                step_token_values,
                prefilled_block_keys.reshape(tokens, full_width),
                prefilled_block_values.reshape(tokens, full_width),
            )
        ]
    )
    slot_shape = jax.ShapeDtypeStruct((slot_count, TOK, PIECE), BF16)
    return pl.pallas_call(
        functools.partial(place_kernel, slot_count),
        out_shape=(
            jax.ShapeDtypeStruct((STEPS, REQUESTS, GROUP * PIECE), F32),
            jax.ShapeDtypeStruct((STEPS, REQUESTS, LOCAL_HEADS * GROUP), F32),
            slot_shape,
            slot_shape,
        ),
        in_specs=[smem] + [vmem] * 4,
        out_specs=(vmem,) * 4,
        compiler_params=pltpu.CompilerParams(vmem_limit_bytes=16 * 2**20),
        name="place",
    )(
        arrival,
        attended,
        norms,
        kc.reshape(n_sp, 2 * TOK, D),
        vc.reshape(n_sp, 2 * TOK, D),
    )


def solution(mesh):
    sp = mesh.shape["sp"]
    n_y = max(2, sp // 16)
    return jax.shard_map(
        functools.partial(on_device, n_y, sp // n_y),
        mesh=mesh,
        in_specs=(
            P(("sp", "tp"), None, None),
            P(("sp", "tp"), None, None),
            P(None, None, "tp"),
            P(None, None, "tp"),
            P(None, None, "tp"),
            P(),
            P(("sp", "tp")),
            P(("sp", "tp")),
            P(("sp", "tp")),
            P(("sp", "tp")),
            P(),
        ),
        out_specs=(
            P(None, None, "tp"),
            P(None, None, "tp"),
            P("sp", None, "tp"),
            P("sp", None, "tp"),
        ),
        check_vma=False,
    )
```

```python
import functools
import math

import jax
import jax.numpy as jnp
from jax import lax
from jax.experimental import pallas as pl
from jax.experimental.pallas import tpu as pltpu
from jax.sharding import PartitionSpec as P

D = 128
TOK = 8
STEPS = 4
REQUESTS = 4
SR = STEPS * REQUESTS
GROUP = 8
ROWS = GROUP * SR
LOCAL_HEADS = 2
PIECE = LOCAL_HEADS * D
NEGATIVE = -1e30
SCALE = 1.0 / math.sqrt(D)
MESH = pl.DeviceIdType.MESH
F32 = jnp.float32
BF16 = jnp.bfloat16
NT = (((1,), (1,)), ((), ()))
TN = (((0,), (0,)), ((), ()))


def exchange_kernel(
    n_y,
    n_zc,
    n_tp,
    own_blocks,
    request_hbm,
    number_hbm,
    rank_hbm,
    slot_hbm,
    lengths_hbm,
    first_hbm,
    q_hbm,
    fresh_k_hbm,
    fresh_v_hbm,
    keys_ref,
    values_ref,
    attended_ref,
    norm_ref,
    arrival_ref,
    kc,
    vc,
    meta,
    kp,
    vp,
    k32,
    v32,
    src_v,
    src_s,
    scores,
    ka,
    kb,
    va,
    vb,
    request_ref,
    number_ref,
    rank_ref,
    slot_ref,
    lengths_ref,
    first_ref,
    q_ref,
    fresh_k_ref,
    fresh_v_ref,
    operand_sem,
    qs,
    fresh_ks,
    fresh_vs,
    sl,
    sy,
    su,
    sv,
    mx,
    my_buf,
    fresh_num,
    rs_src,
    rs_buf,
    yy_buf,
    ag_buf,
    local_sem,
    meta_send,
    meta_recv,
    kp_send,
    kp_recv,
    vp_send,
    vp_recv,
    sl_send,
    sl_recv,
    sy_send,
    sy_recv,
    su_send,
    su_recv,
    sv_send,
    sv_recv,
    mx_send,
    mx_recv,
    my_send,
    my_recv,
    z_send,
    z_recv,
    y_send,
    y_recv,
    rs_send,
    rs_recv,
    yy_send,
    yy_recv,
    ag_send,
    ag_recv,
):
    me = lax.axis_index("sp")
    tp = lax.axis_index("tp")
    my = me // n_zc
    mzc = lax.rem(me, n_zc)
    tokens = own_blocks * TOK

    def zc_at(k):
        return lax.rem(mzc + k, n_zc)

    def y_at(j):
        return lax.rem(my + j, n_y)

    def tp_at(k):
        return lax.rem(tp + k, n_tp)

    z_order = sorted(range(1, n_zc), key=lambda k: -min(k, n_zc - k))
    y_order = sorted(range(1, n_y), key=lambda j: -min(j, n_y - j))
    odd_order = [(j - 1) // 2 for j in y_order if j % 2]
    even_order = [j // 2 for j in y_order if j % 2 == 0]

    def zc_dev(k):
        return (my * n_zc + zc_at(k), tp)

    def y_dev(j):
        return (y_at(j) * n_zc + mzc, tp)

    def tp_dev(k):
        return (me, tp_at(k))

    def remote(src, dst, send, recv, dev):
        copy = pltpu.make_async_remote_copy(
            src_ref=src, dst_ref=dst, send_sem=send, recv_sem=recv, device_id=dev, device_id_type=MESH
        )
        copy.start()
        return copy

    barrier = pltpu.get_barrier_semaphore()
    distant = [(min(k, n_zc - k) // 2, zc_dev(k)) for k in z_order]
    distant += [(min(j, n_y - j), y_dev(j)) for j in y_order]
    distant += [(min(k, n_tp - k), tp_dev(k)) for k in range(1, n_tp)]
    peers = [dev for _, dev in sorted(distant, key=lambda pair: -pair[0])]
    for dev in peers:
        pl.semaphore_signal(barrier, inc=1, device_id=dev, device_id_type=MESH)

    def columns(t):
        return pl.ds(pl.multiple_of(t * PIECE, PIECE), PIECE)

    def rows_of(t):
        return pl.ds(pl.multiple_of(t * tokens, tokens), tokens)

    own_k = pltpu.make_async_copy(keys_ref.at[:, columns(tp)], kp.at[rows_of(tp)], local_sem.at[0])
    own_v = pltpu.make_async_copy(values_ref.at[:, columns(tp)], vp.at[rows_of(tp)], local_sem.at[1])
    own_k.start()
    own_v.start()

    fetches = [
        pltpu.make_async_copy(src, dst, operand_sem.at[n])
        for n, (src, dst) in enumerate(
            (
                (request_hbm, request_ref),
                (number_hbm, number_ref),
                (rank_hbm, rank_ref),
                (slot_hbm, slot_ref),
                (lengths_hbm, lengths_ref),
                (first_hbm, first_ref),
                (q_hbm, q_ref),
                (fresh_k_hbm, fresh_k_ref),
                (fresh_v_hbm, fresh_v_ref),
            )
        )
    ]
    for fetch in fetches:
        fetch.start()
    for fetch in fetches:
        fetch.wait()

    lane = lax.broadcasted_iota(jnp.int32, (1, D), 1)
    codes = jnp.full((1, D), REQUESTS, jnp.int32)
    sources = jnp.zeros((1, D), jnp.int32)
    slots = jnp.zeros((1, D), jnp.int32)
    for b in range(own_blocks):
        request = request_ref[b]
        owner = first_ref[request] + rank_ref[b]
        place = number_ref[b] * TOK + (lane - b * TOK)
        mine = (lane >= b * TOK) & (lane < (b + 1) * TOK) & (place < lengths_ref[request])
        codes = jnp.where(mine, request, codes)
        hit = lane == owner
        sources = jnp.where(hit, tp * own_blocks + b + 1, sources)
        slots = jnp.where(hit, slot_ref[b] + 1, slots)
    own_meta = jnp.concatenate(
        [codes, sources, slots, jnp.zeros((5, D), jnp.int32)], axis=0
    )
    meta[tp] = own_meta

    row_lane = lax.broadcasted_iota(jnp.int32, (1, ROWS), 1)
    row_request = lax.rem(row_lane, REQUESTS)
    row_step = lax.rem(row_lane, SR) // REQUESTS
    row_code = row_request.astype(F32)

    def stack_steps(ref, out):
        out[...] = jnp.concatenate([ref[s].astype(F32) for s in range(STEPS)], axis=0).astype(BF16)

    stack_steps(q_ref, qs)
    stack_steps(fresh_k_ref, fresh_ks)
    stack_steps(fresh_v_ref, fresh_vs)

    def q_head(h):
        return jnp.concatenate(
            [qs[:, pl.ds((h * GROUP + g) * D, D)] for g in range(GROUP)], axis=0
        )

    fresh_row = lax.broadcasted_iota(jnp.int32, (SR, ROWS), 0)
    fresh_ok = (lax.rem(fresh_row, REQUESTS) == row_request) & (fresh_row // REQUESTS <= row_step)
    fresh_scores = []
    for h in range(LOCAL_HEADS):
        dots = lax.dot_general(
            fresh_ks[:, pl.ds(h * D, D)], q_head(h), NT, preferred_element_type=F32
        )
        fresh_scores.append(jnp.where(fresh_ok, dots * SCALE, NEGATIVE))

    k32[0] = jnp.zeros((TOK, PIECE), F32)
    v32[0] = jnp.zeros((TOK, PIECE), F32)

    pl.semaphore_wait(barrier, len(peers))

    x_order = sorted(range(1, n_tp), key=lambda k: -min(k, n_tp - k))
    meta_copies, k_copies, v_copies = [], [], []
    for k in x_order:
        meta_copies.append(
            remote(meta.at[tp], meta.at[tp], meta_send.at[k], meta_recv.at[k], tp_dev(k))
        )
    for k in x_order:
        k_copies.append(
            remote(keys_ref.at[:, columns(tp_at(k))], kp.at[rows_of(tp)], kp_send.at[k], kp_recv.at[k], tp_dev(k))
        )
    for k in x_order:
        v_copies.append(
            remote(
                values_ref.at[:, columns(tp_at(k))], vp.at[rows_of(tp)], vp_send.at[k], vp_recv.at[k], tp_dev(k)
            )
        )

    for copy in meta_copies:
        copy.wait_recv()
    row_meta = meta[0]
    for t in range(1, n_tp):
        row_meta = jnp.maximum(row_meta, meta[t])
    src_v[...] = row_meta
    to_scalar = pltpu.make_async_copy(src_v, src_s, local_sem.at[2])
    to_scalar.start()
    sl[0] = row_meta[2:3, :]
    sl_copies = [
        remote(sl.at[0], sl.at[k], sl_send.at[k], sl_recv.at[k], zc_dev(k)) for k in z_order
    ]
    code_column = jnp.concatenate(
        [
            jnp.transpose(jnp.broadcast_to(meta[t][0:1, :].astype(F32), (D, D)))[:tokens, :]
            for t in range(n_tp)
        ],
        axis=0,
    )
    allowed = code_column == row_code

    own_k.wait()
    for copy in k_copies:
        copy.wait_recv()
    for h in range(LOCAL_HEADS):
        dots = lax.dot_general(kp[:, pl.ds(h * D, D)], q_head(h), NT, preferred_element_type=F32)
        masked = jnp.where(allowed, dots * SCALE, NEGATIVE)
        scores[h] = masked
        mx[0, pl.ds(h, 1), :] = jnp.max(masked, axis=0, keepdims=True)
    mx_copies = [
        remote(mx.at[0], mx.at[k], mx_send.at[k], mx_recv.at[k], zc_dev(k)) for k in z_order
    ]

    def block_tile(ref, index):
        block = ref[index]
        return jnp.concatenate([block[:, :D], block[:, D:]], axis=0).astype(BF16)

    half = n_y // 2
    y_starts = [y_at(j) * n_zc for j in range(n_y)]

    def source_of(k, j):
        return src_s[1, y_starts[j] + zc_at(k)]

    def gather_z(x, staged, k):
        for i in range(half):
            tile = block_tile(staged, source_of(k, 2 * i))
            if isinstance(k, int):
                kb[x, 0, i] = tile
            else:
                ka[x, k, i] = tile

    def gather_y(x, staged, i):
        def step(k, carry):
            va[x, i, k] = block_tile(staged, source_of(k, 2 * i + 1))
            return carry

        lax.fori_loop(0, n_zc, step, 0, unroll=4)

    def z_sends(x, staged, first, last):
        def step(n, carry):
            away = (n + 1) // 2
            k = n_zc // 2 + jnp.where(lax.rem(n, 2) == 1, away, -away)
            gather_z(x, staged, k)
            z_first(x, k).start()
            return carry

        lax.fori_loop(first, last, step, 0)

    def z_first(x, k):
        return pltpu.make_async_remote_copy(
            src_ref=ka.at[x, k],
            dst_ref=kb.at[x, k],
            send_sem=z_send.at[x, 0, k],
            recv_sem=z_recv.at[x, 0, k],
            device_id=zc_dev(k),
            device_id_type=MESH,
        )

    def y_first(x, i):
        return remote(
            va.at[x, i], vb.at[x, i], y_send.at[x, 0, i], y_recv.at[x, 0, i], y_dev(2 * i + 1)
        )

    def y_second(x, out, i):
        return remote(
            kb.at[x, :, i], out.at[0, i], y_send.at[x, 1, i], y_recv.at[x, 1, i], y_dev(2 * i)
        )

    def z_second(x, out, k):
        return remote(
            vb.at[x, :, k], out.at[1, :, k], z_send.at[x, 1, k], z_recv.at[x, 1, k], zc_dev(k)
        )

    local_copies = []

    def keep(src, dst):
        copy = pltpu.make_async_copy(src, dst, local_sem.at[3 + len(local_copies)])
        copy.start()
        local_copies.append(copy)

    k32[pl.ds(1, n_tp * own_blocks)] = kp[...].astype(F32).reshape(n_tp * own_blocks, TOK, PIECE)
    to_scalar.wait()

    ky1, vy1 = [], []
    kz1 = [z_first(0, k) for k in range(1, n_zc)]
    vz1 = [z_first(1, k) for k in range(1, n_zc)]
    per = -(-(n_zc - 1) // half)
    for n, i in enumerate(odd_order):
        gather_y(0, k32, i)
        ky1.append(y_first(0, i))
        z_sends(0, k32, n * per, min(n_zc - 1, (n + 1) * per))
    gather_z(0, k32, 0)

    own_v.wait()
    for copy in v_copies:
        copy.wait_recv()
    v32[pl.ds(1, n_tp * own_blocks)] = vp[...].astype(F32).reshape(n_tp * own_blocks, TOK, PIECE)
    z_sends(1, v32, 0, n_zc - 1)
    gather_z(1, v32, 0)
    for i in range(half):
        gather_y(1, v32, i)

    for copy in mx_copies:
        copy.wait_recv()
    row_max = mx[0]
    for k in range(1, n_zc):
        row_max = jnp.maximum(row_max, mx[k])
    my_buf[0] = row_max
    my_copies = [
        remote(my_buf.at[0], my_buf.at[j], my_send.at[j], my_recv.at[j], y_dev(j)) for j in y_order
    ]
    for i in odd_order:
        vy1.append(y_first(1, i))
    for copy in my_copies:
        copy.wait_recv()
    all_max = my_buf[0]
    for j in range(1, n_y):
        all_max = jnp.maximum(all_max, my_buf[j])

    chunk = D // n_zc
    row_tops = []
    for h in range(LOCAL_HEADS):
        row_top = jnp.maximum(
            all_max[h : h + 1, :], jnp.max(fresh_scores[h], axis=0, keepdims=True)
        )
        row_tops.append(row_top)
        weights = jnp.exp(scores[h] - row_top)
        su[mzc, pl.ds(h, 1), :] = jnp.sum(weights, axis=0, keepdims=True)
        number = lax.dot_general(
            vp[:, pl.ds(h * D, D)], weights.astype(BF16), TN, preferred_element_type=F32
        )
        for p in range(n_zc):
            rs_src[p, pl.ds(h * chunk, chunk), :] = number[p * chunk : (p + 1) * chunk, :]
    rs_copies = [
        remote(rs_src.at[zc_at(k)], rs_buf.at[mzc], rs_send.at[k], rs_recv.at[k], zc_dev(k))
        for k in z_order
    ]
    su_copies = [
        remote(su.at[mzc], su.at[mzc], su_send.at[k], su_recv.at[k], zc_dev(k)) for k in z_order
    ]
    rs_buf[mzc] = rs_src[mzc]

    for copy in kz1:
        copy.wait_recv()
    ky2 = [y_second(0, kc, i) for i in even_order]
    keep(kb.at[0, :, 0], kc.at[0, 0])
    for copy in sl_copies:
        copy.wait_recv()
    for k in range(n_zc):
        sy[0, pl.ds(k, 1), :] = sl[k]
    sy_copies = [
        remote(sy.at[0], sy.at[j], sy_send.at[j], sy_recv.at[j], y_dev(j)) for j in y_order
    ]
    for copy in ky1:
        copy.wait_recv()
    kz2 = [z_second(0, kc, k) for k in z_order]
    keep(vb.at[0, :, 0], kc.at[1, :, 0])

    fresh_totals = []
    for h in range(LOCAL_HEADS):
        weights = jnp.exp(fresh_scores[h] - row_tops[h])
        fresh_totals.append(jnp.sum(weights, axis=0, keepdims=True))
        number = lax.dot_general(
            fresh_vs[:, pl.ds(h * D, D)], weights.astype(BF16), TN, preferred_element_type=F32
        )
        for p in range(n_zc):
            fresh_num[p, pl.ds(h * chunk, chunk), :] = number[p * chunk : (p + 1) * chunk, :]


    for copy in rs_copies:
        copy.wait_recv()
    part = rs_buf[0]
    for p in range(1, n_zc):
        part = part + rs_buf[p]
    yy_buf[my] = part
    yy_copies = [
        remote(yy_buf.at[my], yy_buf.at[my], yy_send.at[j], yy_recv.at[j], y_dev(j)) for j in y_order
    ]
    for copy in su_copies:
        copy.wait_recv()
    part = su[0]
    for p in range(1, n_zc):
        part = part + su[p]
    sv[my] = part
    sv_copies = [
        remote(sv.at[my], sv.at[my], sv_send.at[j], sv_recv.at[j], y_dev(j)) for j in y_order
    ]

    for copy in vz1:
        copy.wait_recv()
    vy2 = [y_second(1, vc, i) for i in even_order]
    keep(kb.at[1, :, 0], vc.at[0, 0])
    for copy in vy1:
        copy.wait_recv()
    vz2 = [z_second(1, vc, k) for k in z_order[: n_zc // 2]]
    keep(vb.at[1, :, 0], vc.at[1, :, 0])

    for copy in yy_copies:
        copy.wait_recv()
    whole = yy_buf[0]
    for copy in sv_copies:
        copy.wait_recv()
    sums = sv[0]
    for j in range(1, n_y):
        whole = whole + yy_buf[j]
        sums = sums + sv[j]
    norms = []
    for h in range(LOCAL_HEADS):
        total = sums[h : h + 1, :] + fresh_totals[h]
        number = whole[h * chunk : (h + 1) * chunk, :] + fresh_num[mzc, pl.ds(h * chunk, chunk), :]
        ag_buf[mzc, pl.ds(h * chunk, chunk), :] = number / total
        norms.append(row_tops[h] + jnp.log(total))
    ag_copies = [
        remote(ag_buf.at[mzc], ag_buf.at[mzc], ag_send.at[k], ag_recv.at[k], zc_dev(k))
        for k in z_order
    ]
    vz2 += [z_second(1, vc, k) for k in z_order[n_zc // 2 :]]
    for copy in sy_copies:
        copy.wait_recv()
    column = []
    for j in range(n_y):
        first_place = (j % 2) * half * n_zc + (j // 2) * n_zc + 1
        lists = sy[j]
        wide = lax.broadcasted_iota(jnp.int32, (n_zc, D), 1)
        picked = jnp.sum(jnp.where(wide == me, lists, 0), axis=1, keepdims=True)
        index = lax.broadcasted_iota(jnp.int32, (n_zc, D), 0) + first_place
        found = jnp.where(picked == wide + 1, index, 0)
        column.append(jnp.max(found, axis=0, keepdims=True))
    arrival = column[0]
    for j in range(1, n_y):
        arrival = jnp.maximum(arrival, column[j])
    arrival_ref[...] = jnp.broadcast_to(arrival, (8, D))
    wide_lane = lax.broadcasted_iota(jnp.int32, (SR, D), 1)
    wide_row = lax.broadcasted_iota(jnp.int32, (SR, D), 0)
    by_head = jnp.zeros((SR, D), F32)
    for h in range(LOCAL_HEADS):
        for g in range(GROUP):
            picked = jnp.where(wide_lane == wide_row + g * SR, norms[h], 0.0)
            value = jnp.sum(picked, axis=1, keepdims=True)
            by_head = jnp.where(wide_lane == h * GROUP + g, value, by_head)
    norm_ref[...] = by_head
    for copy in (
        meta_copies
        + k_copies
        + v_copies
        + sl_copies
        + sy_copies
        + mx_copies
        + my_copies
        + kz1
        + ky1
        + vz1
        + vy1
        + rs_copies
        + su_copies
        + yy_copies
        + sv_copies
    ):
        copy.wait_send()
    for copy in kz2 + ky2:
        copy.wait()
    for copy in ag_copies:
        copy.wait_recv()
    for h in range(LOCAL_HEADS):
        by_entry = jnp.concatenate(
            [ag_buf[p, pl.ds(h * chunk, chunk), :] for p in range(n_zc)], axis=0
        )
        by_row = jnp.transpose(by_entry)
        for g in range(GROUP):
            attended_ref[:, pl.ds((h * GROUP + g) * D, D)] = by_row[g * SR : (g + 1) * SR, :]

    for copy in vz2 + vy2:
        copy.wait_recv()
    for copy in local_copies:
        copy.wait()
    for copy in vz2 + vy2 + ag_copies:
        copy.wait_send()


def place_kernel(
    slot_count,
    arrival_ref,
    rows_ref,
    norm_ref,
    k_ref,
    v_ref,
    attended_ref,
    log_norm_ref,
    out_k_ref,
    out_v_ref,
):
    for s in range(STEPS):
        attended_ref[s] = rows_ref[pl.ds(s * REQUESTS, REQUESTS), :]
        log_norm_ref[s] = norm_ref[pl.ds(s * REQUESTS, REQUESTS), pl.ds(0, LOCAL_HEADS * GROUP)]

    def place(s, carry):
        index = arrival_ref[0, s]
        at = jnp.maximum(index - 1, 0)
        there = index > 0
        for ref, out in ((k_ref, out_k_ref), (v_ref, out_v_ref)):
            tile = ref[at].astype(F32)
            wide = jnp.concatenate([tile[:TOK, :], tile[TOK:, :]], axis=1)
            out[s] = jnp.where(there, wide, 0.0).astype(BF16)
        return carry

    lax.fori_loop(0, slot_count, place, 0, unroll=16)


def on_device(
    n_y,
    n_zc,
    prefilled_block_keys,
    prefilled_block_values,
    queries,
    step_token_keys,
    step_token_values,
    lengths,
    block_request,
    block_number,
    owner_rank,
    owner_slot,
    group_first,
):
    n_tp = lax.axis_size("tp")
    own_blocks, _, full_width = prefilled_block_keys.shape
    row_blocks = own_blocks * n_tp
    tokens = own_blocks * TOK
    slot_count = 2 * row_blocks
    n_sp = n_y * n_zc
    chunk = D // n_zc
    smem = pl.BlockSpec(memory_space=pltpu.SMEM)
    vmem = pl.BlockSpec(memory_space=pltpu.VMEM)
    hbm = pl.BlockSpec(memory_space=pltpu.HBM)
    half = n_y // 2
    dma = pltpu.SemaphoreType.DMA
    attended, norms, arrival, kc, vc = pl.pallas_call(
        functools.partial(exchange_kernel, n_y, n_zc, n_tp, own_blocks),
        out_shape=(
            jax.ShapeDtypeStruct((SR, GROUP * PIECE), F32),
            jax.ShapeDtypeStruct((SR, D), F32),
            jax.ShapeDtypeStruct((8, D), jnp.int32),
            jax.ShapeDtypeStruct((2, half, n_zc, 2 * TOK, D), BF16),
            jax.ShapeDtypeStruct((2, half, n_zc, 2 * TOK, D), BF16),
        ),
        in_specs=[hbm] * 11,
        out_specs=(vmem,) * 5,
        scratch_shapes=[
            pltpu.VMEM((n_tp, 8, D), jnp.int32),
            pltpu.VMEM((n_tp * tokens, PIECE), BF16),
            pltpu.VMEM((n_tp * tokens, PIECE), BF16),
            pltpu.VMEM((row_blocks + 1, TOK, PIECE), F32),
            pltpu.VMEM((row_blocks + 1, TOK, PIECE), F32),
            pltpu.VMEM((8, D), jnp.int32),
            pltpu.SMEM((8, D), jnp.int32),
            pltpu.VMEM((LOCAL_HEADS, n_tp * tokens, ROWS), F32),
            pltpu.VMEM((2, n_zc, half, 2 * TOK, D), BF16),
            pltpu.VMEM((2, n_zc, half, 2 * TOK, D), BF16),
            pltpu.VMEM((2, half, n_zc, 2 * TOK, D), BF16),
            pltpu.VMEM((2, half, n_zc, 2 * TOK, D), BF16),
            pltpu.SMEM((own_blocks,), jnp.int32),
            pltpu.SMEM((own_blocks,), jnp.int32),
            pltpu.SMEM((own_blocks,), jnp.int32),
            pltpu.SMEM((own_blocks,), jnp.int32),
            pltpu.SMEM((REQUESTS,), jnp.int32),
            pltpu.SMEM((REQUESTS,), jnp.int32),
            pltpu.VMEM((STEPS, REQUESTS, GROUP * PIECE), BF16),
            pltpu.VMEM((STEPS, REQUESTS, PIECE), BF16),
            pltpu.VMEM((STEPS, REQUESTS, PIECE), BF16),
            dma((9,)),
            pltpu.VMEM((SR, GROUP * PIECE), BF16),
            pltpu.VMEM((SR, PIECE), BF16),
            pltpu.VMEM((SR, PIECE), BF16),
            pltpu.VMEM((n_zc, 1, D), jnp.int32),
            pltpu.VMEM((n_y, n_zc, D), jnp.int32),
            pltpu.VMEM((n_zc, LOCAL_HEADS, ROWS), F32),
            pltpu.VMEM((n_y, LOCAL_HEADS, ROWS), F32),
            pltpu.VMEM((n_zc, LOCAL_HEADS, ROWS), F32),
            pltpu.VMEM((n_y, LOCAL_HEADS, ROWS), F32),
            pltpu.VMEM((n_zc, LOCAL_HEADS * chunk, ROWS), F32),
            pltpu.VMEM((n_zc, LOCAL_HEADS * chunk, ROWS), F32),
            pltpu.VMEM((n_zc, LOCAL_HEADS * chunk, ROWS), F32),
            pltpu.VMEM((n_y, LOCAL_HEADS * chunk, ROWS), F32),
            pltpu.VMEM((n_zc, LOCAL_HEADS * chunk, ROWS), F32),
            dma((7,)),
        ]
        + [dma((n_tp,))] * 6
        + [dma((n_zc,))] * 2
        + [dma((n_y,))] * 2
        + [dma((n_zc,))] * 2
        + [dma((n_y,))] * 2
        + [dma((n_zc,))] * 2
        + [dma((n_y,))] * 2
        + [dma((2, 2, n_zc))] * 2
        + [dma((2, 2, half))] * 2
        + [dma((n_zc,))] * 2
        + [dma((n_y,))] * 2
        + [dma((n_zc,))] * 2,
        compiler_params=pltpu.CompilerParams(
            collective_id=0, has_side_effects=True, vmem_limit_bytes=40 * 2**20
        ),
        name="exchange",
    )(
        *[
            pltpu.with_memory_space_constraint(operand, pltpu.HBM)
            for operand in (
                block_request,
                block_number,
                owner_rank,
                owner_slot,
                lengths,
                group_first,
                queries,
                step_token_keys,
                step_token_values,
                prefilled_block_keys.reshape(tokens, full_width),
                prefilled_block_values.reshape(tokens, full_width),
            )
        ]
    )
    slot_shape = jax.ShapeDtypeStruct((slot_count, TOK, PIECE), BF16)
    return pl.pallas_call(
        functools.partial(place_kernel, slot_count),
        out_shape=(
            jax.ShapeDtypeStruct((STEPS, REQUESTS, GROUP * PIECE), F32),
            jax.ShapeDtypeStruct((STEPS, REQUESTS, LOCAL_HEADS * GROUP), F32),
            slot_shape,
            slot_shape,
        ),
        in_specs=[smem] + [vmem] * 4,
        out_specs=(vmem,) * 4,
        compiler_params=pltpu.CompilerParams(vmem_limit_bytes=16 * 2**20),
        name="place",
    )(
        arrival,
        attended,
        norms,
        kc.reshape(n_sp, 2 * TOK, D),
        vc.reshape(n_sp, 2 * TOK, D),
    )


def solution(mesh):
    sp = mesh.shape["sp"]
    n_y = max(2, sp // 16)
    return jax.shard_map(
        functools.partial(on_device, n_y, sp // n_y),
        mesh=mesh,
        in_specs=(
            P(("sp", "tp"), None, None),
            P(("sp", "tp"), None, None),
            P(None, None, "tp"),
            P(None, None, "tp"),
            P(None, None, "tp"),
            P(),
            P(("sp", "tp")),
            P(("sp", "tp")),
            P(("sp", "tp")),
            P(("sp", "tp")),
            P(),
        ),
        out_specs=(
            P(None, None, "tp"),
            P(None, None, "tp"),
            P("sp", None, "tp"),
            P("sp", None, "tp"),
        ),
        check_vma=False,
    )
```
